32 devices in a mesh: grp: 2 (over y), ev: 4 (over z), src: 4 (over x, core).
Axes of the slice: x: 2, y: 2, z: 4, core: 2. Of those that a mesh axis runs over, the one named last changes fastest.
Arguments:
- sink_tensor: bfloat16 [4, 256, 256, 256], P('grp', 'ev'), parts along dimension 0, may hold values from -6 to 6
- source_tensor: bfloat16 [4, 2, 256, 256, 256], P('src', None, None, 'ev'), may hold values from -6 to 6
- perambulators: bfloat16 [8, 4, 2, 256, 256], P('src', None, None, 'ev'), may hold values from -0.25 to 0.25
- source_times: int32 [4], replicated, may hold values from 0 to 7, as said below
- spin_index: int32 [2, 3], replicated, may hold values from 0 to 3
Outputs:
- correlator: float32 [4, 4, 2], P('src', 'grp'), parts along dimension 1
The draws below stay inside these ranges and needn't reach their ends.
There are 2 independent parts, one for each index of `grp`. The reference program is written for one: setup_inputs(seed, part) draws one part's arguments, and reference() takes and returns one part's arrays. A program takes and returns all parts, laid end to end along the dimension named above; an argument that names none is the same for every part. Nothing has to cross between parts.
Inputs may be any that keep to these rules, and one draw needn't show every extreme that they name: `source_times`: each contracted source time's perambulator time lies in a block of 2 consecutive times other than block i, where i is the contracted source time's own position.
All inputs are finite; a program needn't handle non-finite values.
Results may differ from the reference program's by a relative error of at most 0.0048.
Values may be sent and summed in bfloat16 or wider, within the bound.
No kernel may reach another device: no remote copies, remote signals or barrier semaphores. Data moves between devices by JAX's collectives and lax.ppermute only.
A program may use at most 256 MiB of HBM per device.

```python
import jax
import jax.numpy as jnp
from jax import lax

N = 256
NS = 4
NSPIN = 2
T0_DEV = 2
NT0 = 8
NSRC = 4


def draw_source_times(key, part):
    key = jax.random.fold_in(key, 11)
    position = jnp.arange(NSRC, dtype=jnp.int32)
    kind_of = position % 3
    offset = jnp.where(kind_of == 0, -1, jnp.where(kind_of == 1, 1, NSRC // 2)).astype(jnp.int32)
    holder = (position + offset + NSRC) % NSRC
    within = jax.random.randint(key, (NSRC,), 0, T0_DEV, dtype=jnp.int32)
    within = jnp.where(position == 0, T0_DEV - 1, within)
    return (holder * T0_DEV + within).astype(jnp.int32)


def set_ends(drawn, rng, smallest, largest):
    shape = drawn.shape
    index_at = [jax.random.randint(jax.random.fold_in(rng, axis), (), 0, shape[axis]) for axis in range(len(shape))]
    drawn = drawn.at[tuple(index_at)].set(smallest)
    longest = shape.index(max(shape))
    index_at[longest] = (index_at[longest] + 1) % shape[longest]
    return drawn.at[tuple(index_at)].set(largest)


def block_levels(stream_key, extent, pieces, smallest, high):
    def one(dim, blocks):
        heights = jax.random.uniform(jax.random.fold_in(jax.random.fold_in(stream_key, 6), dim), (blocks,), jnp.float32, smallest / len(pieces), high / len(pieces))
        return jnp.repeat(jnp.exp(heights), extent[dim] // blocks).reshape((-1,) + (1,) * (len(extent) - dim - 1))

    gain = one(*pieces[0])
    for cut in pieces[1:]:
        gain = gain * one(*cut)
    return gain


def gaussian(rng, dims, deviation, reach, split=(), held_as=jnp.bfloat16):
    result = deviation * jax.random.normal(rng, dims, jnp.float32)
    if split:
        result = result * block_levels(rng, dims, split, -0.22, 0.18)
    return jnp.clip(result, -reach, reach).astype(held_as)


def setup_inputs(seed: int = 0, part: int = 0) -> dict:
    seeds = jax.random.split(jax.random.key(seed), 6)
    part_keys = jax.random.split(jax.random.fold_in(seeds[5], part), 6)
    sink_tensor = gaussian(part_keys[0], (2, N, N, N), 1.0, 6.0, ((1, 4),))
    source_tensor = gaussian(seeds[1], (NSRC, 2, N, N, N), 1.0, 6.0, ((0, 4), (3, 4)))
    perambulators = gaussian(seeds[2], (NT0, NS, 2, N, N), (2 * N) ** -0.5, 0.25, ((0, 4), (3, 4)))
    source_times = draw_source_times(jax.random.fold_in(seeds[5], 71), part)
    spin_index = set_ends(jax.random.randint(seeds[4], (NSPIN, 3), 0, NS), jax.random.fold_in(seeds[4], 1), 0, NS - 1).astype(jnp.int32)
    return dict(sink_tensor=sink_tensor, source_tensor=source_tensor, perambulators=perambulators, source_times=source_times, spin_index=spin_index)


def apply_mode(tensor, matrix, pattern):
    tensor = tensor.astype(jnp.float32)
    matrix = matrix.astype(jnp.float32)
    first = jnp.einsum(pattern, tensor[0], matrix[0], precision=lax.Precision.HIGHEST)
    second = jnp.einsum(pattern, tensor[1], matrix[1], precision=lax.Precision.HIGHEST)
    third = jnp.einsum(pattern, tensor[0], matrix[1], precision=lax.Precision.HIGHEST)
    fourth = jnp.einsum(pattern, tensor[1], matrix[0], precision=lax.Precision.HIGHEST)
    return jnp.stack([first - second, third + fourth])


def inner_product(sink_side, source_side):
    source_side = source_side.astype(jnp.float32)
    real_part = jnp.sum(sink_side[0] * source_side[0] + sink_side[1] * source_side[1])
    imag_part = jnp.sum(sink_side[1] * source_side[0] - sink_side[0] * source_side[1])
    return jnp.stack([real_part, imag_part])


def reference(sink_tensor, source_tensor, perambulators, source_times, spin_index):
    scale = float(N) ** -1.5

    def one_source(position):
        chosen = lax.dynamic_index_in_dim(source_times, position, 0, keepdims=False).astype(jnp.int32)
        per_time = lax.dynamic_index_in_dim(perambulators, chosen, 0, keepdims=False)
        source_side = lax.dynamic_index_in_dim(source_tensor, position, 0, keepdims=False)
        results = []
        for structure in range(NSPIN):
            first_map = lax.dynamic_index_in_dim(per_time, spin_index[structure, 0].astype(jnp.int32), 0, keepdims=False)
            second_map = lax.dynamic_index_in_dim(per_time, spin_index[structure, 1].astype(jnp.int32), 0, keepdims=False)
            third_map = lax.dynamic_index_in_dim(per_time, spin_index[structure, 2].astype(jnp.int32), 0, keepdims=False)
            after_last = apply_mode(sink_tensor, third_map, "abc,cd->abd").astype(jnp.bfloat16)
            after_middle = apply_mode(after_last, second_map, "abc,bd->adc").astype(jnp.bfloat16)
            sink_side = apply_mode(after_middle, first_map, "abc,ad->dbc")
            results.append(inner_product(sink_side, source_side) * scale)
        return jnp.stack(results)

    return lax.map(one_source, jnp.arange(NSRC, dtype=jnp.int32))
```

```python
import functools

import jax
import jax.numpy as jnp
from jax import lax
from jax.experimental import pallas as pl
from jax.experimental.pallas import tpu as pltpu
from jax.sharding import PartitionSpec as P

BF16, F32 = jnp.bfloat16, jnp.float32
LANES = 128
BLOCK = 8


def project_kernel(left_ref, source_ref, out_ref):
    structures, _, halves, _, rows, lanes = out_ref.shape
    for i in range(source_ref.shape[0]):
        got = jnp.dot(left_ref[...], source_ref[i], preferred_element_type=F32)
        for h in range(halves):
            out_ref[:, :, h, i] = got[:, h * lanes : (h + 1) * lanes].reshape(structures, 2, rows, lanes)


def project_source(left, source, structures):
    e, k, n = source.shape
    rows = left.shape[0] // (2 * structures)
    halves = n // LANES
    per = 4
    return pl.pallas_call(
        project_kernel,
        grid=(e // per,),
        in_specs=[
            pl.BlockSpec(left.shape, lambda i: (0, 0)),
            pl.BlockSpec((per, k, n), lambda i: (i, 0, 0)),
        ],
        out_specs=pl.BlockSpec((structures, 2, halves, per, rows, LANES), lambda i: (0, 0, 0, i, 0, 0)),
        out_shape=jax.ShapeDtypeStruct((structures, 2, halves, e, rows, LANES), F32),
        compiler_params=pltpu.CompilerParams(vmem_limit_bytes=48 * 1024 * 1024),
        cost_estimate=pl.CostEstimate(
            flops=2 * left.shape[0] * k * n * e,
            bytes_accessed=2 * source.size + 4 * left.shape[0] * e * n,
            transcendentals=0,
        ),
        name="project_source",
    )(left, source)


def contract_kernel(at_ref, sink_ref, *refs, sources):
    t_refs, (q_ref, w_ref, acc_ref, out_ref) = refs[:sources], refs[sources:]
    _, block, n, _ = sink_ref.shape
    structures, _, halves, e, _, lanes = t_refs[0].shape

    @pl.when(pl.program_id(0) == 0)
    def _():
        out_ref[...] = acc_ref[...]

    @pl.when(at_ref[2] > 0)
    def _():
        re_rows = sink_ref[0].reshape(block * n, n)
        im_rows = sink_ref[1].reshape(block * n, n)
        for g in range(sources):
            t_rows = t_refs[g].reshape(structures * 2 * halves * e * block, lanes)
            for s in range(structures):
                c = g * structures + s
                acc = [[jnp.zeros((8, lanes), F32) for _ in range(halves)] for _ in range(2)]
                first = jnp.dot(re_rows, w_ref[c, 0], preferred_element_type=F32)
                first += jnp.dot(im_rows, w_ref[c, 1], preferred_element_type=F32)
                first = first.astype(BF16)
                for a in range(block):
                    one = first[a * n : (a + 1) * n]
                    second = jnp.dot(q_ref[c, 0], one[:, :n], preferred_element_type=F32)
                    second += jnp.dot(q_ref[c, 1], one[:, n:], preferred_element_type=F32)
                    second = second.astype(BF16).astype(F32)
                    for h in range(halves):
                        re = second[:e, h * lanes : (h + 1) * lanes]
                        im = second[e:, h * lanes : (h + 1) * lanes]
                        base = (s * 2 * halves + h) * e * block + a
                        tre = t_rows[pl.ds(base, e, stride=block), :]
                        tim = t_rows[pl.ds(base + halves * e * block, e, stride=block), :]
                        acc[0][h] += (re * tre - im * tim).reshape(e // 8, 8, lanes).sum(0)
                        acc[1][h] += (re * tim + im * tre).reshape(e // 8, 8, lanes).sum(0)
                for part in range(2):
                    for h in range(halves):
                        out_ref[c, part, h] += acc[part][h]


def contract(sink, sink_block, ts, t_block, valid, q, w, acc, blocks):
    n = sink.shape[2]
    structures, _, halves, e, _, lanes = ts[0].shape
    whole = lambda ref: pl.BlockSpec(ref.shape, lambda i, at: (0,) * ref.ndim)
    at = jnp.stack([jnp.asarray(v, jnp.int32) for v in (sink_block, t_block, valid)])
    combos = w.shape[0]
    return pl.pallas_call(
        functools.partial(contract_kernel, sources=len(ts)),
        grid_spec=pltpu.PrefetchScalarGridSpec(
            num_scalar_prefetch=1,
            grid=(blocks,),
            in_specs=[pl.BlockSpec((2, BLOCK, n, n), lambda i, at: (0, at[0] + i, 0, 0))]
            + [pl.BlockSpec((structures, 2, halves, e, BLOCK, lanes), lambda i, at: (0, 0, 0, 0, at[1] + i, 0))] * len(ts)
            + [whole(q), whole(w), whole(acc)],
            out_specs=whole(acc),
        ),
        out_shape=jax.ShapeDtypeStruct(acc.shape, F32),
        compiler_params=pltpu.CompilerParams(vmem_limit_bytes=56 * 1024 * 1024),
        cost_estimate=pl.CostEstimate(
            flops=blocks * BLOCK * combos * 2 * (n * 2 * n * 2 * n + 2 * e * 2 * n * n),
            bytes_accessed=blocks * BLOCK * (4 * n * n + combos * 8 * e * n),
            transcendentals=0,
        ),
        name="contract",
    )(at, sink, *ts, q, w, acc)


def own_maps(perambulators, source_times):
    position, srcs = lax.axis_index("src"), lax.axis_size("src")
    held = perambulators.shape[0]
    own_time = lax.dynamic_index_in_dim(source_times, position, 0, keepdims=False)
    chosen = None
    for k in range(1, srcs):
        to = lax.rem(position + srcs - k, srcs)
        within = lax.dynamic_index_in_dim(source_times, to, 0, keepdims=False) - position * held
        within = jnp.clip(within, 0, held - 1)
        sent = lax.dynamic_index_in_dim(perambulators, within, 0, keepdims=False)
        got = lax.ppermute(sent, "src", [(j, (j + srcs - k) % srcs) for j in range(srcs)])
        here = own_time // held == lax.rem(position + k, srcs)
        chosen = got if chosen is None else jnp.where(here, got, chosen)
    return lax.all_gather(chosen, "ev", axis=2, tiled=True)


def pick(per_time, spin):
    return lax.dynamic_index_in_dim(per_time, spin, 0, keepdims=False)


def left_of(per_time, spin_index, rows):
    out = []
    for s in range(spin_index.shape[0]):
        p = rows(pick(per_time, spin_index[s, 0]))
        out += [jnp.concatenate([p[0], p[1]], 1), jnp.concatenate([p[1], -p[0]], 1)]
    return jnp.concatenate(out, 0)


def middle_of(per_time, spin_index, ev, e):
    out = []
    for s in range(spin_index.shape[0]):
        p = pick(per_time, spin_index[s, 1])
        p = lax.dynamic_slice_in_dim(p, ev * e, e, axis=2).transpose(0, 2, 1)
        out.append(jnp.stack([jnp.concatenate([p[0], p[1]], 0), jnp.concatenate([-p[1], p[0]], 0)]))
    return jnp.stack(out)


def right_of(per_time, spin_index):
    out = []
    for s in range(spin_index.shape[0]):
        p = pick(per_time, spin_index[s, 2])
        out.append(jnp.stack([jnp.concatenate([p[0], p[1]], 1), jnp.concatenate([-p[1], p[0]], 1)]))
    return jnp.stack(out)


def body_any(sink_tensor, source_tensor, perambulators, source_times, spin_index):
    position, ev = lax.axis_index("src"), lax.axis_index("ev")
    evs, srcs = lax.axis_size("ev"), lax.axis_size("src")
    structures = spin_index.shape[0]
    _, slice_a, n, _ = sink_tensor.shape
    e = n // evs
    share = slice_a // srcs
    mine = lax.dynamic_slice_in_dim(sink_tensor, position * share, share, axis=1)
    sink = lax.all_gather(mine, ("ev", "src"), axis=1, tiled=True)
    per_time = own_maps(perambulators, source_times)
    source = source_tensor[0].reshape(2 * n, e, n).transpose(1, 0, 2)
    t = project_source(left_of(per_time, spin_index, lambda p: p), source, structures)
    q, w = middle_of(per_time, spin_index, ev, e), right_of(per_time, spin_index)
    acc = jnp.zeros((structures, 2, n // LANES, 8, LANES), F32)
    acc = contract(sink, 0, [t], 0, 1, q, w, acc, n // BLOCK)
    return lax.psum(acc.sum((2, 3, 4)), "ev")


def body_relay(sink_tensor, source_tensor, perambulators, source_times, spin_index):
    position, ev, grp = lax.axis_index("src"), lax.axis_index("ev"), lax.axis_index("grp")
    evs, srcs = lax.axis_size("ev"), lax.axis_size("src")
    structures = spin_index.shape[0]
    _, slice_a, n, _ = sink_tensor.shape
    e = n // evs
    chip, core = position // 2, position % 2
    half = slice_a // 2
    units = half // BLOCK
    is_end = (ev == 0) | (ev == evs - 1)
    is_inner = jnp.logical_not(is_end)
    near = jnp.where(ev < 2, 1 - ev, 5 - ev)
    opposite = 3 - ev
    across = 3 - near

    def unit(w):
        return jnp.where(chip == 0, w, units - 1 - w)

    def partner_unit(w):
        return jnp.where(chip == 0, units - 1 - w, w)

    def own(w):
        return lax.dynamic_slice_in_dim(sink_tensor, core * half + BLOCK * unit(w), BLOCK, axis=1)

    both = lambda v: lax.ppermute(v, "ev", [(0, 1), (1, 0), (2, 3), (3, 2)])
    outward = lambda v: lax.ppermute(v, "ev", [(1, 0), (2, 3)])
    inward = lambda v: lax.ppermute(v, "ev", [(0, 1), (3, 2)])
    middle = lambda v: lax.ppermute(v, "ev", [(1, 2), (2, 1)])
    swap_chips = lambda v: lax.ppermute(v, "src", [(0, 2), (2, 0), (1, 3), (3, 1)])
    swap_cores = lambda v: lax.ppermute(v, "src", [(0, 1), (1, 0), (2, 3), (3, 2)])
    swap_groups = lambda v: lax.ppermute(v, "grp", [(0, 1), (1, 0)])

    own0, own1, own2 = own(0), own(1), own(2)
    a1, b1 = both(own0), middle(own0)
    per_time = own_maps(perambulators, source_times)
    source = source_tensor[0].reshape(2 * n, e, n).transpose(1, 0, 2)
    other_source = swap_cores(source)
    other_time = swap_cores(per_time)

    rows = lambda p: lax.dynamic_index_in_dim(p.reshape(2, evs, 2, half, n), core, 2, keepdims=False).reshape(2, n // 2, n)
    times = (per_time, other_time)
    ts = [
        project_source(left_of(p, spin_index, rows), src, structures)
        for p, src in zip(times, (source, other_source))
    ]
    q = jnp.concatenate([middle_of(p, spin_index, ev, e) for p in times])
    q_near = jnp.concatenate([middle_of(p, spin_index, near, e) for p in times])
    w = jnp.concatenate([right_of(p, spin_index) for p in times])
    acc = jnp.zeros((2 * structures, 2, n // LANES, 8, LANES), F32)

    x1 = swap_chips(a1)
    b2 = middle(a1)
    a2 = both(jnp.where(is_end, own1, b1))
    x2 = swap_chips(jnp.where(is_end, a2, b1))
    b3 = middle(own1)
    a3 = both(jnp.where(is_end, own2, b2))
    x3 = swap_chips(jnp.where(is_end, a3, b2))
    b4 = middle(a2)
    a4 = outward(b3)
    x4 = swap_chips(jnp.where(is_end, a4, b3))
    a5 = outward(b4)
    x5 = swap_chips(jnp.where(is_end, a5, b4))
    block = near * units + 1 + grp
    sent = jnp.stack([lax.dynamic_slice_in_dim(t, block * BLOCK, BLOCK, axis=4) for t in ts]).astype(BF16)
    near_t = inward(sent)
    far_t = swap_groups(near_t)

    def add(acc, unit_array, end_slice, inner_slice, end_unit, inner_unit, valid=1):
        t_block = jnp.where(is_end, end_slice * units + end_unit, inner_slice * units + inner_unit)
        return contract(unit_array, 0, ts, t_block, valid, q, w, acc, 1)

    acc = contract(sink_tensor, core * units, ts, ev * units, 1, q, w, acc, units)
    acc = add(acc, a1, near, near, unit(0), unit(0))
    acc = add(acc, b1, 0, opposite, 0, unit(0), is_inner)
    acc = add(acc, a2, across, near, unit(0), unit(1))
    acc = add(acc, b2, 0, across, 0, unit(0), is_inner)
    acc = add(acc, x1, near, near, partner_unit(0), partner_unit(0))
    acc = add(acc, a3, opposite, near, unit(0), unit(2))
    acc = add(acc, b3, 0, opposite, 0, unit(1), is_inner)
    acc = add(acc, x2, across, opposite, partner_unit(0), partner_unit(0))
    acc = add(acc, a4, across, 0, unit(1), 0, is_end)
    acc = add(acc, b4, 0, across, 0, unit(1), is_inner)
    acc = add(acc, x3, opposite, across, partner_unit(0), partner_unit(0))
    for received, which in ((near_t, grp), (far_t, 1 - grp)):
        wide = [received[g].astype(F32) for g in range(2)]
        acc = contract(sink_tensor, core * units + 1 + which, wide, 0, is_inner, q_near, w, acc, 1)
    acc = add(acc, a5, opposite, 0, unit(1), 0, is_end)
    acc = add(acc, x4, across, opposite, partner_unit(1), partner_unit(1))
    acc = add(acc, x5, opposite, across, partner_unit(1), partner_unit(1))

    part = acc.sum((2, 3, 4)).reshape(2, structures, 2)
    each = jnp.arange(srcs)[:, None, None]
    placed = jnp.where(each == position, part[0], 0.0) + jnp.where(each == position + 1 - 2 * core, part[1], 0.0)
    return lax.psum(placed, ("ev", "src"))[position]


def body(relay, *args):
    totals = (body_relay if relay else body_any)(*args)
    return (totals * float(args[0].shape[3]) ** -1.5)[None]


def solution(mesh):
    relay = mesh.shape["ev"] == 4 and mesh.shape["src"] == 4 and mesh.shape["grp"] == 2
    in_specs = (
        P("grp", "ev", None, None),
        P("src", None, None, "ev", None),
        P("src", None, None, "ev", None),
        P(),
        P(),
    )
    out_specs = P("src", "grp", None)
    return jax.shard_map(functools.partial(body, relay), mesh=mesh, in_specs=in_specs, out_specs=out_specs, check_vma=False)
```

```python
import functools

import jax
import jax.numpy as jnp
import numpy as np
from jax import lax
from jax.experimental import pallas as pl
from jax.experimental.pallas import tpu as pltpu
from jax.sharding import PartitionSpec as P

BF16, F32 = jnp.bfloat16, jnp.float32
LANES = 128
BLOCK = 8


def project_kernel(left_ref, source_ref, out_ref, wide_ref):
    structures, _, halves, per, rows, lanes = out_ref.shape
    parts, n = source_ref.shape[:2]
    for part in range(parts):
        for h in range(halves):
            one = source_ref[part, :, :, h * lanes : (h + 1) * lanes]
            wide_ref[part, h] = one.astype(F32).reshape(n * per, lanes)
    for i in range(per):
        one = [
            jnp.concatenate([wide_ref[part, h, pl.ds(i, n, stride=per), :].astype(BF16) for h in range(halves)], 1)
            for part in range(parts)
        ]
        got = jnp.dot(left_ref[...], jnp.concatenate(one, 0), preferred_element_type=F32)
        for h in range(halves):
            out_ref[:, :, h, i] = got[:, h * lanes : (h + 1) * lanes].reshape(structures, 2, rows, lanes)


def project_source(left, source, structures):
    parts, _, e, n = source.shape
    rows = left.shape[0] // (2 * structures)
    halves = n // LANES
    per = min(16, e)
    return pl.pallas_call(
        project_kernel,
        grid=(e // per,),
        in_specs=[
            pl.BlockSpec(left.shape, lambda i: (0, 0)),
            pl.BlockSpec((parts, n, per, n), lambda i: (0, 0, i, 0)),
        ],
        out_specs=pl.BlockSpec((structures, 2, halves, per, rows, LANES), lambda i: (0, 0, 0, i, 0, 0)),
        out_shape=jax.ShapeDtypeStruct((structures, 2, halves, e, rows, LANES), F32),
        scratch_shapes=[pltpu.VMEM((parts, halves, n * per, LANES), F32)],
        compiler_params=pltpu.CompilerParams(vmem_limit_bytes=56 * 1024 * 1024),
        cost_estimate=pl.CostEstimate(
            flops=2 * left.shape[0] * 2 * n * n * e,
            bytes_accessed=2 * source.size + 4 * left.shape[0] * e * n,
            transcendentals=0,
        ),
        name="project_source",
    )(left, source)


def contract_block(sink, t_views, q_ref, w_ref, out_ref, e):
    _, block, n, _ = sink.shape
    combos, _, halves, _, lanes = out_ref.shape
    structures = combos // len(t_views)
    re_rows = sink[0].reshape(block * n, n)
    im_rows = sink[1].reshape(block * n, n)
    for g, t_rows in enumerate(t_views):
        for s in range(structures):
            c = g * structures + s
            acc = [[jnp.zeros((8, lanes), F32) for _ in range(halves)] for _ in range(2)]
            first = jnp.dot(re_rows, w_ref[c, 0], preferred_element_type=F32)
            first += jnp.dot(im_rows, w_ref[c, 1], preferred_element_type=F32)
            first = first.astype(BF16)
            for a in range(block):
                one = first[a * n : (a + 1) * n]
                second = jnp.dot(q_ref[c, 0], one[:, :n], preferred_element_type=F32)
                second += jnp.dot(q_ref[c, 1], one[:, n:], preferred_element_type=F32)
                second = second.astype(BF16).astype(F32)
                for h in range(halves):
                    re = second[:e, h * lanes : (h + 1) * lanes]
                    im = second[e:, h * lanes : (h + 1) * lanes]
                    base = (s * 2 * halves + h) * e * block + a
                    tre = t_rows[pl.ds(base, e, stride=block), :]
                    tim = t_rows[pl.ds(base + halves * e * block, e, stride=block), :]
                    acc[0][h] += (re * tre - im * tim).reshape(e // 8, 8, lanes).sum(0)
                    acc[1][h] += (re * tim + im * tre).reshape(e // 8, 8, lanes).sum(0)
            for part in range(2):
                for h in range(halves):
                    out_ref[c, part, h] += acc[part][h]


def t_view(ref):
    structures, _, halves, e, block, lanes = ref.shape
    return ref.reshape(structures * 2 * halves * e * block, lanes)


def contract_kernel(at_ref, sink_ref, *refs, sources, base):
    t_refs, (q_ref, w_ref, acc_ref, out_ref) = refs[:sources], refs[sources:]
    e = t_refs[0].shape[3]

    @pl.when(pl.program_id(0) == 0)
    def _():
        out_ref[...] = acc_ref[...]

    @pl.when(at_ref[base + 2] > 0)
    def _():
        contract_block(sink_ref, [t_view(t) for t in t_refs], q_ref, w_ref, out_ref, e)


def whole(ref):
    return pl.BlockSpec(ref.shape, lambda i, at: (0,) * ref.ndim)


def t_specs(ts, block_at):
    structures, _, halves, e, _, lanes = ts[0].shape
    shape = (structures, 2, halves, e, BLOCK, lanes)
    return [pl.BlockSpec(shape, lambda i, at: (0, 0, 0, 0, block_at(i, at), 0))] * len(ts)


def contract_cost(blocks, combos, n, e):
    return pl.CostEstimate(
        flops=blocks * BLOCK * combos * 2 * (n * 2 * n * 2 * n + 2 * e * 2 * n * n),
        bytes_accessed=blocks * BLOCK * (4 * n * n + combos * 8 * e * n),
        transcendentals=0,
    )


def scalars(*values):
    return jnp.stack([jnp.asarray(v, jnp.int32) for v in values])


def contract(sink, ts, table, base, q, w, acc, blocks):
    n = sink.shape[2]
    return pl.pallas_call(
        functools.partial(contract_kernel, sources=len(ts), base=base),
        grid_spec=pltpu.PrefetchScalarGridSpec(
            num_scalar_prefetch=1,
            grid=(blocks,),
            in_specs=[pl.BlockSpec((2, BLOCK, n, n), lambda i, at: (0, at[base] + i, 0, 0))]
            + t_specs(ts, lambda i, at: at[base + 1] + i)
            + [whole(q), whole(w), whole(acc)],
            out_specs=whole(acc),
        ),
        out_shape=jax.ShapeDtypeStruct(acc.shape, F32),
        compiler_params=pltpu.CompilerParams(vmem_limit_bytes=56 * 1024 * 1024),
        cost_estimate=contract_cost(blocks, w.shape[0], n, ts[0].shape[3]),
        name="contract",
    )(table, sink, *ts, q, w, acc)


def slots_kernel(at_ref, *refs, sources, shapes, base):
    arrays = sum(len(parts) for choices in shapes for parts in choices)
    sinks, refs = refs[:arrays], refs[arrays:]
    t_refs, (q_ref, w_ref, acc_ref, out_ref, held, sem) = refs[:sources], refs[sources:]
    e = t_refs[0].shape[3]
    i = pl.program_id(0)

    def fetch(slot):
        place = sum(len(parts) for choices in shapes[:slot] for parts in choices)
        for k, parts in enumerate(shapes[slot]):

            @pl.when(at_ref[base + 2 * slot] == k + 1)
            def _():
                row = 0
                for part, size in enumerate(parts):
                    to = held.at[slot % 2, :, pl.ds(row, size)]
                    pltpu.make_async_copy(sinks[place + part], to, sem.at[slot % 2]).start()
                    row += size

            place += len(parts)

    @pl.when(i == 0)
    def _():
        fetch(0)
        out_ref[...] = acc_ref[...]

    for slot in range(1, len(shapes)):

        @pl.when(i == slot - 1)
        def _():
            fetch(slot)

    @pl.when(at_ref[base + 2 * i] > 0)
    def _():
        now = lax.rem(i, 2)
        pltpu.make_async_copy(held.at[now], held.at[now], sem.at[now]).wait()
        contract_block(held.at[now], [t_view(t) for t in t_refs], q_ref, w_ref, out_ref, e)


def contract_slots(slots, ts, table, base, q, w, acc):
    n = q.shape[-1]
    arrays = [part for choices in slots for parts in choices for part in parts]
    shapes = tuple(tuple(tuple(part.shape[1] for part in parts) for parts in choices) for choices in slots)
    return pl.pallas_call(
        functools.partial(slots_kernel, sources=len(ts), shapes=shapes, base=base),
        grid_spec=pltpu.PrefetchScalarGridSpec(
            num_scalar_prefetch=1,
            grid=(len(slots),),
            in_specs=[pl.BlockSpec(memory_space=pl.ANY)] * len(arrays)
            + t_specs(ts, lambda i, at: at[base + 2 * i + 1])
            + [whole(q), whole(w), whole(acc)],
            out_specs=whole(acc),
            scratch_shapes=[pltpu.VMEM((2, 2, BLOCK, n, n), BF16), pltpu.SemaphoreType.DMA((2,))],
        ),
        out_shape=jax.ShapeDtypeStruct(acc.shape, F32),
        compiler_params=pltpu.CompilerParams(vmem_limit_bytes=56 * 1024 * 1024),
        cost_estimate=contract_cost(len(slots), w.shape[0], n, ts[0].shape[3]),
        name="contract_slots",
    )(table, *arrays, *ts, q, w, acc)


def near_kernel(at_ref, sink_ref, t_ref, q_ref, w_ref, acc_ref, out_ref, wide_ref, *, base):
    out_ref[...] = acc_ref[...]
    e = q_ref.shape[2] // 2

    @pl.when(at_ref[base + 1] > 0)
    def _():
        sources = t_ref.shape[0]
        wide_ref[...] = t_ref[...].reshape(wide_ref.shape).astype(F32)
        rows = wide_ref.shape[1]
        contract_block(sink_ref, [wide_ref.at[g] for g in range(sources)], q_ref, w_ref, out_ref, e)


def contract_near(sink, t, table, base, q, w, acc):
    n = sink.shape[2]
    return pl.pallas_call(
        functools.partial(near_kernel, base=base),
        grid_spec=pltpu.PrefetchScalarGridSpec(
            num_scalar_prefetch=1,
            grid=(1,),
            in_specs=[pl.BlockSpec((2, BLOCK, n, n), lambda i, at: (0, at[base], 0, 0)), whole(t), whole(q), whole(w), whole(acc)],
            out_specs=whole(acc),
            scratch_shapes=[pltpu.VMEM((t.shape[0], t.size // t.shape[0] // LANES, LANES), F32)],
        ),
        out_shape=jax.ShapeDtypeStruct(acc.shape, F32),
        compiler_params=pltpu.CompilerParams(vmem_limit_bytes=56 * 1024 * 1024),
        cost_estimate=contract_cost(1, w.shape[0], n, q.shape[2] // 2),
        name="contract_near",
    )(table, sink, t, q, w, acc)


def after(value, *others):
    return lax.optimization_barrier((value, *others))[0]


def rows_to_send(perambulators, source_times):
    position, srcs = lax.axis_index("src"), lax.axis_size("src")
    held = perambulators.shape[0]
    out = []
    for k in range(1, srcs):
        to = lax.rem(position + srcs - k, srcs)
        within = lax.dynamic_index_in_dim(source_times, to, 0, keepdims=False) - position * held
        out.append(lax.dynamic_index_in_dim(perambulators, jnp.clip(within, 0, held - 1), 0, keepdims=False))
    return out


def own_rows(sent, held, source_times):
    position, srcs = lax.axis_index("src"), lax.axis_size("src")
    own_time = lax.dynamic_index_in_dim(source_times, position, 0, keepdims=False)
    chosen = None
    for k in range(1, srcs):
        got = lax.ppermute(sent[k - 1], "src", [(j, (j + srcs - k) % srcs) for j in range(srcs)])
        here = own_time // held == lax.rem(position + k, srcs)
        chosen = got if chosen is None else jnp.where(here, got, chosen)
    return chosen


def all_rows(rows):
    return lax.all_gather(rows, "ev", axis=2, tiled=True)


def maps_kernel(at_ref, *refs, sources, chunks, stride, e):
    times, (left_ref, right_ref, *middle_refs, turned) = refs[:sources], refs[sources:]
    _, parts, n, _ = times[0].shape
    structures = right_ref.shape[0] // sources
    size = left_ref.shape[1] // (structures * 2 * chunks)
    start = at_ref[3 * structures]
    for g in range(sources):
        for s in range(structures):
            first, second, third = (times[g].at[at_ref[3 * s + k]] for k in range(3))
            for k in range(chunks):
                rows = pl.ds(pl.multiple_of(start + k * stride, size), size)
                re, im = first[0, rows, :], first[1, rows, :]
                for part, (x, y) in enumerate(((re, im), (im, -re))):
                    to = ((s * 2 + part) * chunks + k) * size
                    left_ref[g, to : to + size, :n] = x
                    left_ref[g, to : to + size, n:] = y
            c = g * structures + s
            re, im = third[0], third[1]
            right_ref[c, 0, :, :n] = re
            right_ref[c, 0, :, n:] = im
            right_ref[c, 1, :, :n] = -im
            right_ref[c, 1, :, n:] = re
            for part in range(parts):
                turned[part] = second[part].astype(F32).T
            for k, middle_ref in enumerate(middle_refs):
                columns = pl.ds(pl.multiple_of(at_ref[3 * structures + 1 + k], e), e)
                re, im = turned[0, columns, :], turned[1, columns, :]
                middle_ref[c, 0] = jnp.concatenate([re, im], 0).astype(BF16)
                middle_ref[c, 1] = jnp.concatenate([-im, re], 0).astype(BF16)


def maps(times, spin_index, first_row, chunks, size, stride, e, places):
    n = times[0].shape[2]
    structures, sources = spin_index.shape[0], len(times)
    combos = sources * structures
    at = jnp.concatenate([spin_index.reshape(-1), scalars(first_row, *places)])
    shapes = [(sources, structures * 2 * chunks * size, 2 * n), (combos, 2, n, 2 * n)] + [(combos, 2, 2 * e, n)] * len(places)
    return pl.pallas_call(
        functools.partial(maps_kernel, sources=sources, chunks=chunks, stride=stride, e=e),
        grid_spec=pltpu.PrefetchScalarGridSpec(
            num_scalar_prefetch=1,
            grid=(1,),
            in_specs=[whole(t) for t in times],
            out_specs=[pl.BlockSpec(shape, lambda i, at, d=len(shape): (0,) * d) for shape in shapes],
            scratch_shapes=[pltpu.VMEM((2, n, n), F32)],
        ),
        out_shape=[jax.ShapeDtypeStruct(shape, BF16) for shape in shapes],
        compiler_params=pltpu.CompilerParams(vmem_limit_bytes=48 * 1024 * 1024),
        name="maps",
    )(at, *times)


def body_any(sink_tensor, source_tensor, perambulators, source_times, spin_index):
    position, ev = lax.axis_index("src"), lax.axis_index("ev")
    evs, srcs = lax.axis_size("ev"), lax.axis_size("src")
    structures = spin_index.shape[0]
    _, slice_a, n, _ = sink_tensor.shape
    e = n // evs
    share = slice_a // srcs
    mine = lax.dynamic_slice_in_dim(sink_tensor, position * share, share, axis=1)
    sink = lax.all_gather(mine, ("ev", "src"), axis=1, tiled=True)
    sent = rows_to_send(perambulators, source_times)
    per_time = all_rows(own_rows(sent, perambulators.shape[0], source_times))
    left, w, q = maps([per_time], spin_index, 0, 1, n, n, e, [ev * e])
    t = project_source(left[0], source_tensor[0], structures)
    acc = jnp.zeros((structures, 2, n // LANES, 8, LANES), F32)
    acc = contract(sink, [t], scalars(0, 0, 1), 0, q, w, acc, n // BLOCK)
    return lax.psum(acc.sum((2, 3, 4)), "ev")


RELAY_CALLS = (
    (
        (("near", "u0"), None, 1),
        (None, ("opposite", "u0"), 1),
        (("near", "p0"), ("opposite", "p0"), 1),
    ),
    (
        (("across", "u0"), ("near", "u0"), 2),
        (None, ("opposite", "u1"), 1),
    ),
    (
        (("across", "p0"), ("near", "p0"), 1),
        (("across", "u1"), ("near", "u1"), 2),
    ),
    (
        (("opposite", "u0"), ("across", "u0"), 2),
        (("across", "p1"), ("opposite", "p1"), 1),
    ),
    (
        (None, ("near", "u2"), 1),
        (("opposite", "p0"), ("across", "p0"), 1),
        (("opposite", "u1"), ("across", "u1"), 2),
    ),
    ((("opposite", "p1"), ("across", "p1"), 2),),
)
OWN_TABLE = 10
BASES = tuple(OWN_TABLE + 2 * sum(len(call) for call in RELAY_CALLS[:k]) for k in range(len(RELAY_CALLS)))


def relay_table(evs, units):
    rows = []
    for ev in range(evs):
        for position in range(4):
            for grp in range(2):
                chip, core = position // 2, position % 2
                end = int(ev in (0, evs - 1))
                near = 1 - ev if ev < 2 else 5 - ev
                slices = dict(near=near, opposite=3 - ev, across=3 - near)
                unit = {f"u{w}": units - 1 - w if chip else w for w in range(units)}
                unit |= {f"p{w}": w if chip else units - 1 - w for w in range(units)}
                row = [core * units, ev * units, 1]
                row += [core * units + units // 2, ev * units + units // 2, 1]
                row += [core * units + 1 + grp, 1 - end, core * units + 2 - grp, 1 - end]
                for call in RELAY_CALLS:
                    for at_end, at_inner, choices in call:
                        at = at_end if end else at_inner
                        which = 0 if at is None else 1 if end or choices == 1 else 2
                        row += [which, 0 if at is None else slices[at[0]] * units + unit[at[1]]]
                rows.append(row)
    return np.array(rows, np.int32)


def body_relay(sink_tensor, source_tensor, perambulators, source_times, spin_index):
    position, ev, grp = lax.axis_index("src"), lax.axis_index("ev"), lax.axis_index("grp")
    evs, srcs = lax.axis_size("ev"), lax.axis_size("src")
    structures = spin_index.shape[0]
    _, slice_a, n, _ = sink_tensor.shape
    e = n // evs
    chip, core = position // 2, position % 2
    half = slice_a // 2
    units = half // BLOCK
    is_end = (ev == 0) | (ev == evs - 1)
    near = jnp.where(ev < 2, 1 - ev, 5 - ev)

    def unit(w):
        return jnp.where(chip == 0, w, units - 1 - w)

    def own(w, start=0, size=BLOCK):
        return lax.dynamic_slice_in_dim(sink_tensor, core * half + BLOCK * unit(w) + start, size, axis=1)

    outward = lambda v: lax.ppermute(v, "ev", [(1, 0), (2, 3)])
    inward = lambda v: lax.ppermute(v, "ev", [(0, 1), (3, 2)])
    middle = lambda v: lax.ppermute(v, "ev", [(1, 2), (2, 1)])
    swap_chips = lambda v: lax.ppermute(v, "src", [(0, 2), (2, 0), (1, 3), (3, 1)])
    swap_cores = lambda v: lax.ppermute(v, "src", [(0, 1), (1, 0), (2, 3), (3, 2)])
    swap_groups = lambda v: lax.ppermute(v, "grp", [(0, 1), (1, 0)])

    table = jnp.asarray(relay_table(evs, units))
    table = lax.dynamic_index_in_dim(table, (ev * 4 + position) * 2 + grp, 0, keepdims=False)
    base1, base2, base3, base4, base5, base6 = BASES

    choose = lambda a, b: jnp.where(is_end, a, b)

    sent = rows_to_send(perambulators, source_times)
    rows_here = own_rows(sent, perambulators.shape[0], source_times)
    spins = rows_here.shape[0]
    small = BLOCK // 4
    own0s, own0r, own2a, own2b = own(0, 0, small), own(0, small, BLOCK - small), own(2, 0, BLOCK // 2), own(2, BLOCK // 2, BLOCK // 2)
    own0, own1 = own(0), own(1)
    rows_here = after(rows_here, own0s, own0r, own2a, own2b, own0, own1)
    some = lax.dynamic_slice_in_dim(rows_here, grp * (spins // 2), spins // 2, axis=0)
    mine = jnp.stack([lax.ppermute(some, "ev", [(j, (j + k) % evs) for j in range(evs)]) for k in range(1, evs)])
    q1s, b1s, e1a = outward(own0s), middle(own0s), inward(own2a)
    others = swap_groups(after(mine, q1s, b1s))
    q1r, b1r, e2, b3 = outward(own0r), middle(own0r), inward(own0), middle(own1)
    whole_rows = jnp.where(grp == 0, jnp.concatenate([mine, others], 1), jnp.concatenate([others, mine], 1))
    whole_rows = [rows_here if k == 0 else whole_rows[k - 1] for k in range(evs)]
    turned = jnp.stack([whole_rows[(evs - 1 - k) % evs] for k in range(2 * evs - 1)])
    turned = lax.dynamic_slice_in_dim(turned, evs - 1 - ev, evs, axis=0)
    per_time = turned.transpose(1, 2, 0, 3, 4).reshape(spins, 2, n, n)
    other_time = swap_cores(per_time)
    source = source_tensor[0]
    other_source = swap_cores(after(source, rows_here))
    lefts, w, q, q_near = maps(
        [per_time, other_time], spin_index, core * half, evs, half, slice_a, e, [ev * e, near * e]
    )
    acc = jnp.zeros((2 * structures, 2, n // LANES, 8, LANES), F32)
    join = lambda *parts: jnp.concatenate(parts, 1)

    t_own = project_source(lefts[0], source, structures)
    q1r, b1r = after((q1r, b1r), t_own)
    b1, q1 = join(b1s, b1r), join(q1s, q1r)
    q2 = outward(b1)
    x1 = swap_chips(choose(q1, b1))
    e3, e1b = inward(after(own1, t_own)), inward(after(own2b, t_own))
    t_other = project_source(lefts[1], after(other_source, t_own, b1, q1), structures)
    ts = (t_own, t_other)
    block = near * units + 1 + grp
    to_near = jnp.stack([lax.dynamic_slice_in_dim(t, block * BLOCK, BLOCK, axis=4) for t in ts]).astype(BF16)
    near_t = inward(to_near.reshape(to_near.shape[:4] + (e * BLOCK, LANES)))
    acc = contract(sink_tensor, ts, table, 0, q, w, acc, units // 2)
    q3 = outward(after(b3, acc))
    x2 = swap_chips(choose(after(q2, acc), e2))
    b2 = middle(after(e2, acc))
    acc = contract(sink_tensor, ts, table, 3, q, w, after(acc, b3, q2, e2), units // 2)
    acc = contract_slots([[(q1,)], [(b1,)], [(x1,)]], ts, table, base1, q, w, acc)
    q4 = outward(after(b2, acc))
    x3 = swap_chips(choose(after(q3, acc), b3))
    b4 = middle(after(e3, acc))
    b5 = middle(after(e1a, acc))
    acc = contract_slots([[(q2,), (e2,)], [(b3,)]], ts, table, base2, q, w, after(acc, b2, q3, e3))
    far_t = swap_groups(after(near_t, acc))
    acc = contract_slots([[(x2,)], [(q3,), (e3,)]], ts, table, base3, q, w, after(acc, near_t))
    q5 = outward(after(b4, acc))
    x4 = swap_chips(choose(after(q4, acc), b2))
    acc = contract_near(sink_tensor, near_t, table, 6, q_near, w, after(acc, b4, q4))
    q6 = outward(after(b5, acc))
    acc = contract_near(sink_tensor, far_t, table, 8, q_near, w, after(acc, b5))
    acc = contract_slots([[(q4,), (b2,)], [(x3,)]], ts, table, base4, q, w, acc)
    x5 = swap_chips(choose(after(q5, acc), b4)[:, BLOCK // 2 :])
    acc = contract_slots([[(e1a, e1b)], [(x4,)], [(q5,), (b4,)]], ts, table, base5, q, w, after(acc, q5))
    acc = contract_slots([[(q6, x5), (b5, x5)]], ts, table, base6, q, w, acc)

    part = acc.sum((2, 3, 4)).reshape(2, structures, 2)
    total = part[0] + swap_cores(part[1])
    return lax.psum(total, "ev")


def body(relay, *args):
    totals = (body_relay if relay else body_any)(*args)
    return (totals * float(args[0].shape[3]) ** -1.5)[None]


def solution(mesh):
    relay = mesh.shape["ev"] == 4 and mesh.shape["src"] == 4 and mesh.shape["grp"] == 2
    in_specs = (
        P("grp", "ev", None, None),
        P("src", None, None, "ev", None),
        P("src", None, None, "ev", None),
        P(),
        P(),
    )
    out_specs = P("src", "grp", None)
    return jax.shard_map(functools.partial(body, relay), mesh=mesh, in_specs=in_specs, out_specs=out_specs, check_vma=False)
```

```python
import functools

import jax
import jax.numpy as jnp
import numpy as np
from jax import lax
from jax.experimental import pallas as pl
from jax.experimental.pallas import tpu as pltpu
from jax.sharding import PartitionSpec as P

BF16, F32 = jnp.bfloat16, jnp.float32
LANES = 128
BLOCK = 8


def project_kernel(at_ref, left_ref, source_ref, *refs):
    out_ref, near_ref, wide_ref = refs[-3:]
    structures, _, halves, per, rows, lanes = out_ref.shape
    parts, n = source_ref.shape[:2]
    for part in range(parts):
        for h in range(halves):
            one = source_ref[part, :, :, h * lanes : (h + 1) * lanes]
            wide_ref[part, h] = one.astype(F32).reshape(n * per, lanes)
    for i in range(per):
        one = [
            jnp.concatenate([wide_ref[part, h, pl.ds(i, n, stride=per), :].astype(BF16) for h in range(halves)], 1)
            for part in range(parts)
        ]
        got = jnp.dot(left_ref[...], jnp.concatenate(one, 0), preferred_element_type=F32)
        for h in range(halves):
            out_ref[:, :, h, i] = got[:, h * lanes : (h + 1) * lanes].reshape(structures, 2, rows, lanes)
    block = out_ref[:, :, :, :, pl.ds(pl.multiple_of(at_ref[0] * BLOCK, BLOCK), BLOCK), :]
    near_ref[0] = block.reshape(structures, 2, halves, per * BLOCK, lanes).astype(BF16)


def project_source(left, source, structures, block, near, place):
    parts, _, e, n = source.shape
    rows = left.shape[0] // (2 * structures)
    halves = n // LANES
    per = min(16, e)
    near_block = (1, structures, 2, halves, per * BLOCK, LANES)
    return pl.pallas_call(
        project_kernel,
        grid_spec=pltpu.PrefetchScalarGridSpec(
            num_scalar_prefetch=1,
            grid=(e // per,),
            in_specs=[
                pl.BlockSpec(left.shape, lambda i, at: (0, 0)),
                pl.BlockSpec((parts, n, per, n), lambda i, at: (0, 0, i, 0)),
            ]
            + ([] if near is None else [pl.BlockSpec(memory_space=pl.ANY)]),
            out_specs=[
                pl.BlockSpec((structures, 2, halves, per, rows, LANES), lambda i, at: (0, 0, 0, i, 0, 0)),
                pl.BlockSpec(near_block, lambda i, at: (place, 0, 0, 0, i, 0)),
            ],
            scratch_shapes=[pltpu.VMEM((parts, halves, n * per, LANES), F32)],
        ),
        out_shape=[
            jax.ShapeDtypeStruct((structures, 2, halves, e, rows, LANES), F32),
            jax.ShapeDtypeStruct((2, structures, 2, halves, e * BLOCK, LANES), BF16),
        ],
        input_output_aliases={} if near is None else {3: 1},
        compiler_params=pltpu.CompilerParams(vmem_limit_bytes=49 * 1024 * 1024),
        cost_estimate=pl.CostEstimate(
            flops=2 * left.shape[0] * 2 * n * n * e,
            bytes_accessed=2 * source.size + 4 * left.shape[0] * e * n,
            transcendentals=0,
        ),
        name="project_source",
    )(scalars(block), left, source, *([] if near is None else [near]))


def contract_block(sink, t_views, q_ref, w_ref, out_ref, e):
    _, block, n, _ = sink.shape
    combos, _, halves, _, lanes = out_ref.shape
    structures = combos // len(t_views)
    group = block // 2
    for g, t_rows in enumerate(t_views):
        for s in range(structures):
            c = g * structures + s
            acc = [[jnp.zeros((8, lanes), F32) for _ in range(halves)] for _ in range(2)]
            for start in range(0, block, group):
                rows = [sink[part, start : start + group].reshape(group * n, n) for part in range(2)]
                first = jnp.dot(jnp.concatenate(rows, 1), w_ref[c], preferred_element_type=F32)
                first = first.astype(BF16)
                for a in range(group):
                    one = first[a * n : (a + 1) * n]
                    one = jnp.concatenate([one[:, :n], one[:, n:]], 0)
                    second = jnp.dot(q_ref[c], one, preferred_element_type=F32)
                    second = second.astype(BF16).astype(F32)
                    for h in range(halves):
                        re = second[:e, h * lanes : (h + 1) * lanes]
                        im = second[e:, h * lanes : (h + 1) * lanes]
                        base = (s * 2 * halves + h) * e * block + start + a
                        tre = t_rows[pl.ds(base, e, stride=block), :]
                        tim = t_rows[pl.ds(base + halves * e * block, e, stride=block), :]
                        acc[0][h] += (re * tre - im * tim).reshape(e // 8, 8, lanes).sum(0)
                        acc[1][h] += (re * tim + im * tre).reshape(e // 8, 8, lanes).sum(0)
            for part in range(2):
                for h in range(halves):
                    out_ref[c, part, h] += acc[part][h]


def t_view(ref):
    structures, _, halves, e, block, lanes = ref.shape
    return ref.reshape(structures * 2 * halves * e * block, lanes)


def contract_kernel(at_ref, sink_ref, *refs, sources, base):
    t_refs, (q_ref, w_ref, acc_ref, out_ref) = refs[:sources], refs[sources:]
    e = t_refs[0].shape[3]

    @pl.when(pl.program_id(0) == 0)
    def _():
        out_ref[...] = acc_ref[...]

    @pl.when(at_ref[base + 2] > 0)
    def _():
        contract_block(sink_ref, [t_view(t) for t in t_refs], q_ref, w_ref, out_ref, e)


def whole(ref):
    return pl.BlockSpec(ref.shape, lambda i, at: (0,) * ref.ndim)


def t_specs(ts, block_at):
    structures, _, halves, e, _, lanes = ts[0].shape
    shape = (structures, 2, halves, e, BLOCK, lanes)
    return [pl.BlockSpec(shape, lambda i, at: (0, 0, 0, 0, block_at(i, at), 0))] * len(ts)


def contract_cost(blocks, combos, n, e):
    return pl.CostEstimate(
        flops=blocks * BLOCK * combos * 2 * (n * 2 * n * 2 * n + 2 * e * 2 * n * n),
        bytes_accessed=blocks * BLOCK * (4 * n * n + combos * 8 * e * n),
        transcendentals=0,
    )


def scalars(*values):
    return jnp.stack([jnp.asarray(v, jnp.int32) for v in values])


def contract(sink, ts, table, base, q, w, acc, blocks):
    n = sink.shape[2]
    return pl.pallas_call(
        functools.partial(contract_kernel, sources=len(ts), base=base),
        grid_spec=pltpu.PrefetchScalarGridSpec(
            num_scalar_prefetch=1,
            grid=(blocks,),
            in_specs=[pl.BlockSpec((2, BLOCK, n, n), lambda i, at: (0, at[base] + i, 0, 0))]
            + t_specs(ts, lambda i, at: at[base + 1] + i)
            + [whole(q), whole(w), whole(acc)],
            out_specs=whole(acc),
        ),
        out_shape=jax.ShapeDtypeStruct(acc.shape, F32),
        compiler_params=pltpu.CompilerParams(vmem_limit_bytes=49 * 1024 * 1024),
        cost_estimate=contract_cost(blocks, w.shape[0], n, ts[0].shape[3]),
        name="contract",
    )(table, sink, *ts, q, w, acc)


def slots_kernel(at_ref, *refs, sources, shapes, base):
    arrays = sum(len(parts) for choices in shapes for parts in choices)
    sinks, refs = refs[:arrays], refs[arrays:]
    t_refs, (q_ref, w_ref, acc_ref, out_ref, held, sem) = refs[:sources], refs[sources:]
    e = t_refs[0].shape[3]
    i = pl.program_id(0)

    def fetch(slot):
        place = sum(len(parts) for choices in shapes[:slot] for parts in choices)
        for k, parts in enumerate(shapes[slot]):

            @pl.when(at_ref[base + 2 * slot] == k + 1)
            def _():
                row = 0
                for part, size in enumerate(parts):
                    to = held.at[slot % 2, :, pl.ds(row, size)]
                    pltpu.make_async_copy(sinks[place + part], to, sem.at[slot % 2]).start()
                    row += size

            place += len(parts)

    @pl.when(i == 0)
    def _():
        fetch(0)
        out_ref[...] = acc_ref[...]

    for slot in range(1, len(shapes)):

        @pl.when(i == slot - 1)
        def _():
            fetch(slot)

    @pl.when(at_ref[base + 2 * i] > 0)
    def _():
        now = lax.rem(i, 2)
        pltpu.make_async_copy(held.at[now], held.at[now], sem.at[now]).wait()
        contract_block(held.at[now], [t_view(t) for t in t_refs], q_ref, w_ref, out_ref, e)


def contract_slots(slots, ts, table, base, q, w, acc):
    n = q.shape[2] // 2
    arrays = [part for choices in slots for parts in choices for part in parts]
    shapes = tuple(tuple(tuple(part.shape[1] for part in parts) for parts in choices) for choices in slots)
    return pl.pallas_call(
        functools.partial(slots_kernel, sources=len(ts), shapes=shapes, base=base),
        grid_spec=pltpu.PrefetchScalarGridSpec(
            num_scalar_prefetch=1,
            grid=(len(slots),),
            in_specs=[pl.BlockSpec(memory_space=pl.ANY)] * len(arrays)
            + t_specs(ts, lambda i, at: at[base + 2 * i + 1])
            + [whole(q), whole(w), whole(acc)],
            out_specs=whole(acc),
            scratch_shapes=[pltpu.VMEM((2, 2, BLOCK, n, n), BF16), pltpu.SemaphoreType.DMA((2,))],
        ),
        out_shape=jax.ShapeDtypeStruct(acc.shape, F32),
        compiler_params=pltpu.CompilerParams(vmem_limit_bytes=49 * 1024 * 1024),
        cost_estimate=contract_cost(len(slots), w.shape[0], n, ts[0].shape[3]),
        name="contract_slots",
    )(table, *arrays, *ts, q, w, acc)


def near_kernel(at_ref, sink_ref, t_ref, other_ref, q_ref, w_ref, acc_ref, out_ref, wide_ref, *, base):
    e = q_ref.shape[1] // 2
    i = pl.program_id(0)

    @pl.when(i == 0)
    def _():
        out_ref[...] = acc_ref[...]

    @pl.when(at_ref[base + 2] > 0)
    def _():
        sources = t_ref.shape[0]

        @pl.when(i == 0)
        def _():
            wide_ref[...] = t_ref[...].reshape(wide_ref.shape).astype(F32)

        @pl.when(i == 1)
        def _():
            wide_ref[...] = other_ref[...].reshape(wide_ref.shape).astype(F32)

        contract_block(sink_ref, [wide_ref.at[g] for g in range(sources)], q_ref, w_ref, out_ref, e)


def contract_near(sink, t, other, table, base, q, w, acc):
    n = sink.shape[2]
    return pl.pallas_call(
        functools.partial(near_kernel, base=base),
        grid_spec=pltpu.PrefetchScalarGridSpec(
            num_scalar_prefetch=1,
            grid=(2,),
            in_specs=[pl.BlockSpec((2, BLOCK, n, n), lambda i, at: (0, at[base + i], 0, 0))]
            + [whole(t), whole(other), whole(q), whole(w), whole(acc)],
            out_specs=whole(acc),
            scratch_shapes=[pltpu.VMEM((t.shape[0], t.size // t.shape[0] // LANES, LANES), F32)],
        ),
        out_shape=jax.ShapeDtypeStruct(acc.shape, F32),
        compiler_params=pltpu.CompilerParams(vmem_limit_bytes=49 * 1024 * 1024),
        cost_estimate=contract_cost(2, w.shape[0], n, q.shape[1] // 2),
        name="contract_near",
    )(table, sink, t, other, q, w, acc)


def after(value, *others):
    return lax.optimization_barrier((value, *others))[0]


def rows_to_send(perambulators, source_times):
    position, srcs = lax.axis_index("src"), lax.axis_size("src")
    held = perambulators.shape[0]
    out = []
    for k in range(1, srcs):
        to = lax.rem(position + srcs - k, srcs)
        within = lax.dynamic_index_in_dim(source_times, to, 0, keepdims=False) - position * held
        out.append(lax.dynamic_index_in_dim(perambulators, jnp.clip(within, 0, held - 1), 0, keepdims=False))
    return out


def own_rows(sent, held, source_times):
    position, srcs = lax.axis_index("src"), lax.axis_size("src")
    own_time = lax.dynamic_index_in_dim(source_times, position, 0, keepdims=False)
    chosen = None
    for k in range(1, srcs):
        got = lax.ppermute(sent[k - 1], "src", [(j, (j + srcs - k) % srcs) for j in range(srcs)])
        here = own_time // held == lax.rem(position + k, srcs)
        chosen = got if chosen is None else jnp.where(here, got, chosen)
    return chosen


def all_rows(rows):
    return lax.all_gather(rows, "ev", axis=2, tiled=True)


def maps_kernel(at_ref, *refs, sources, chunks, stride, e):
    times, left_refs, (right_ref, *middle_refs, turned) = refs[:sources], refs[sources : 2 * sources], refs[2 * sources :]
    _, parts, n, _ = times[0].shape
    structures = right_ref.shape[0] // sources
    size = left_refs[0].shape[0] // (structures * 2 * chunks)
    start = at_ref[3 * structures]
    for g in range(sources):
        for s in range(structures):
            first, second, third = (times[g].at[at_ref[3 * s + k]] for k in range(3))
            for k in range(chunks):
                rows = pl.ds(pl.multiple_of(start + k * stride, size), size)
                re, im = first[0, rows, :], first[1, rows, :]
                for part, (x, y) in enumerate(((re, im), (im, -re))):
                    to = ((s * 2 + part) * chunks + k) * size
                    left_refs[g][to : to + size, :n] = x
                    left_refs[g][to : to + size, n:] = y
            c = g * structures + s
            re, im = third[0], third[1]
            right_ref[c, :n, :n] = re
            right_ref[c, :n, n:] = im
            right_ref[c, n:, :n] = -im
            right_ref[c, n:, n:] = re
            for part in range(parts):
                turned[part] = second[part].astype(F32).T
            for k, middle_ref in enumerate(middle_refs):
                columns = pl.ds(pl.multiple_of(at_ref[3 * structures + 1 + k], e), e)
                re, im = turned[0, columns, :], turned[1, columns, :]
                middle_ref[c, :, :n] = jnp.concatenate([re, im], 0).astype(BF16)
                middle_ref[c, :, n:] = jnp.concatenate([-im, re], 0).astype(BF16)


def maps(times, spin_index, first_row, chunks, size, stride, e, places):
    n = times[0].shape[2]
    structures, sources = spin_index.shape[0], len(times)
    combos = sources * structures
    at = jnp.concatenate([spin_index.reshape(-1), scalars(first_row, *places)])
    shapes = [(structures * 2 * chunks * size, 2 * n)] * sources + [(combos, 2 * n, 2 * n)] + [(combos, 2 * e, 2 * n)] * len(places)
    return pl.pallas_call(
        functools.partial(maps_kernel, sources=sources, chunks=chunks, stride=stride, e=e),
        grid_spec=pltpu.PrefetchScalarGridSpec(
            num_scalar_prefetch=1,
            grid=(1,),
            in_specs=[whole(t) for t in times],
            out_specs=[pl.BlockSpec(shape, lambda i, at, d=len(shape): (0,) * d) for shape in shapes],
            scratch_shapes=[pltpu.VMEM((2, n, n), F32)],
        ),
        out_shape=[jax.ShapeDtypeStruct(shape, BF16) for shape in shapes],
        compiler_params=pltpu.CompilerParams(vmem_limit_bytes=48 * 1024 * 1024),
        name="maps",
    )(at, *times)


def body_any(sink_tensor, source_tensor, perambulators, source_times, spin_index):
    position, ev = lax.axis_index("src"), lax.axis_index("ev")
    evs, srcs = lax.axis_size("ev"), lax.axis_size("src")
    structures = spin_index.shape[0]
    _, slice_a, n, _ = sink_tensor.shape
    e = n // evs
    share = slice_a // srcs
    mine = lax.dynamic_slice_in_dim(sink_tensor, position * share, share, axis=1)
    sink = lax.all_gather(mine, ("ev", "src"), axis=1, tiled=True)
    sent = rows_to_send(perambulators, source_times)
    per_time = all_rows(own_rows(sent, perambulators.shape[0], source_times))
    left, w, q = maps([per_time], spin_index, 0, 1, n, n, e, [ev * e])
    t, _ = project_source(left, source_tensor[0], structures, 0, None, 0)
    acc = jnp.zeros((structures, 2, n // LANES, 8, LANES), F32)
    acc = contract(sink, [t], scalars(0, 0, 1), 0, q, w, acc, n // BLOCK)
    return lax.psum(acc.sum((2, 3, 4)), "ev")


RELAY_CALLS = (
    (
        (("near", "u0"), None, 1),
        (None, ("opposite", "u0"), 1),
        (("near", "p0"), ("opposite", "p0"), 1),
    ),
    (
        (("across", "u0"), ("near", "u0"), 2),
        (None, ("opposite", "u1"), 1),
    ),
    (
        (("across", "p0"), ("near", "p0"), 1),
        (("across", "u1"), ("near", "u1"), 2),
    ),
    (
        (("opposite", "u0"), ("across", "u0"), 2),
        (("across", "p1"), ("opposite", "p1"), 1),
        (None, ("near", "u2"), 1),
    ),
    (
        (("opposite", "p0"), ("across", "p0"), 1),
        (("opposite", "u1"), ("across", "u1"), 2),
    ),
    ((("opposite", "p1"), ("across", "p1"), 2),),
)
OWN_TABLE = 9
BASES = tuple(OWN_TABLE + 2 * sum(len(call) for call in RELAY_CALLS[:k]) for k in range(len(RELAY_CALLS)))


def relay_table(evs, units):
    rows = []
    for ev in range(evs):
        for position in range(4):
            for grp in range(2):
                chip, core = position // 2, position % 2
                end = int(ev in (0, evs - 1))
                near = 1 - ev if ev < 2 else 5 - ev
                slices = dict(near=near, opposite=3 - ev, across=3 - near)
                unit = {f"u{w}": units - 1 - w if chip else w for w in range(units)}
                unit |= {f"p{w}": w if chip else units - 1 - w for w in range(units)}
                row = [core * units, ev * units, 1]
                row += [core * units + units // 2, ev * units + units // 2, 1]
                row += [core * units + 1 + grp, core * units + 2 - grp, 1 - end]
                for call in RELAY_CALLS:
                    for at_end, at_inner, choices in call:
                        at = at_end if end else at_inner
                        which = 0 if at is None else 1 if end or choices == 1 else 2
                        row += [which, 0 if at is None else slices[at[0]] * units + unit[at[1]]]
                rows.append(row)
    return np.array(rows, np.int32)


def body_relay(sink_tensor, source_tensor, perambulators, source_times, spin_index):
    position, ev, grp = lax.axis_index("src"), lax.axis_index("ev"), lax.axis_index("grp")
    evs, srcs = lax.axis_size("ev"), lax.axis_size("src")
    structures = spin_index.shape[0]
    _, slice_a, n, _ = sink_tensor.shape
    e = n // evs
    chip, core = position // 2, position % 2
    half = slice_a // 2
    units = half // BLOCK
    is_end = (ev == 0) | (ev == evs - 1)
    near = jnp.where(ev < 2, 1 - ev, 5 - ev)

    def unit(w):
        return jnp.where(chip == 0, w, units - 1 - w)

    def own(w, start=0, size=BLOCK):
        return lax.dynamic_slice_in_dim(sink_tensor, core * half + BLOCK * unit(w) + start, size, axis=1)

    outward = lambda v: lax.ppermute(v, "ev", [(1, 0), (2, 3)])
    inward = lambda v: lax.ppermute(v, "ev", [(0, 1), (3, 2)])
    middle = lambda v: lax.ppermute(v, "ev", [(1, 2), (2, 1)])
    swap_chips = lambda v: lax.ppermute(v, "src", [(0, 2), (2, 0), (1, 3), (3, 1)])
    swap_cores = lambda v: lax.ppermute(v, "src", [(0, 1), (1, 0), (2, 3), (3, 2)])
    swap_groups = lambda v: lax.ppermute(v, "grp", [(0, 1), (1, 0)])

    table = jnp.asarray(relay_table(evs, units))
    table = lax.dynamic_index_in_dim(table, (ev * 4 + position) * 2 + grp, 0, keepdims=False)
    base1, base2, base3, base4, base5, base6 = BASES

    choose = lambda a, b: jnp.where(is_end, a, b)

    sent = rows_to_send(perambulators, source_times)
    rows_here = own_rows(sent, perambulators.shape[0], source_times)
    spins = rows_here.shape[0]
    small = BLOCK // 4
    own0s = own(0, 0, small)
    q1s, b1s = outward(own0s), middle(own0s)
    own0, own0r = own(0), own(0, small, BLOCK - small)
    rows_here = after(rows_here, q1s, b1s, own0, own0r, table)
    some = lax.dynamic_slice_in_dim(rows_here, grp * (spins // 2), spins // 2, axis=0)
    mine = jnp.stack([lax.ppermute(some, "ev", [(j, (j + k) % evs) for j in range(evs)]) for k in range(1, evs)])
    own1, own2a, own2b = own(1), own(2, 0, BLOCK // 2), own(2, BLOCK // 2, BLOCK // 2)
    others = swap_groups(after(mine, own1, own2a, own2b))
    whole_rows = jnp.where(grp == 0, jnp.concatenate([mine, others], 1), jnp.concatenate([others, mine], 1))
    whole_rows = [rows_here if k == 0 else whole_rows[k - 1] for k in range(evs)]
    turned = jnp.stack([whole_rows[(evs - 1 - k) % evs] for k in range(2 * evs - 1)])
    turned = lax.dynamic_slice_in_dim(turned, evs - 1 - ev, evs, axis=0)
    per_time = turned.transpose(1, 2, 0, 3, 4).reshape(spins, 2, n, n)
    other_time = swap_cores(per_time)
    source = source_tensor[0]
    other_source = swap_cores(after(source, rows_here))
    *lefts, w, q, q_near = maps(
        [per_time, other_time], spin_index, core * half, evs, half, slice_a, e, [ev * e, near * e]
    )
    own0r, own0, own1 = after((own0r, own0, own1), mine)
    q1r, b1r, e2, b3 = outward(own0r), middle(own0r), inward(own0), middle(own1)
    acc = jnp.zeros((2 * structures, 2, n // LANES, 8, LANES), F32)
    join = lambda *parts: jnp.concatenate(parts, 1)

    block = near * units + 1 + grp
    t_own, to_near = project_source(lefts[0], source, structures, block, None, 0)
    q1r, b1r = after((q1r, b1r), t_own)
    b1, q1 = join(b1s, b1r), join(q1s, q1r)
    q2 = outward(b1)
    out1 = choose(q1, b1)
    x1 = swap_chips(out1)
    e3, e1a, e1b = inward(after(own1, out1)), inward(after(own2a, out1)), inward(after(own2b, out1))
    t_other, to_near = project_source(lefts[1], after(other_source, t_own, b1, q1, out1), structures, block, to_near, 1)
    ts = (t_own, t_other)
    b2 = middle(after(e2, t_other))
    acc = contract(sink_tensor, ts, table, 0, q, w, after(acc, e2), units // 2)
    q3 = outward(after(b3, acc))
    out2 = choose(after(q2, acc), e2)
    x2 = swap_chips(out2)
    acc = contract(sink_tensor, ts, table, 3, q, w, after(acc, out2, x1), units // 2)
    near_t = inward(after(to_near, acc))
    q4 = outward(after(b2, acc))
    b4 = middle(after(e3, acc))
    acc = contract_slots([[(q1,)], [(b1,)], [(x1,)]], ts, table, base1, q, w, after(acc, b2, e3, e1a))
    out3 = choose(after(q3, acc), b3)
    x3 = swap_chips(out3)
    b5 = middle(after(e1a, acc))
    acc = contract_slots([[(q2,), (e2,)], [(b3,)]], ts, table, base2, q, w, after(acc, out3, x2))
    far_t = swap_groups(after(near_t, acc))
    q5 = outward(after(b4, acc))
    acc = contract_slots([[(x2,)], [(q3,), (e3,)]], ts, table, base3, q, w, after(acc, b4, near_t))
    out4 = choose(after(q4, acc), b2)
    x4 = swap_chips(out4)
    q6 = outward(after(b5, acc))
    acc = contract_slots([[(q4,), (b2,)], [(x3,)], [(e1a, e1b)]], ts, table, base4, q, w, after(acc, out4, b5))
    acc = contract_near(sink_tensor, near_t, far_t, table, 6, q_near, w, acc)
    out5 = choose(after(q5, acc), b4)[:, BLOCK // 2 :]
    x5 = swap_chips(out5)
    acc = contract_slots([[(x4,)], [(q5,), (b4,)]], ts, table, base5, q, w, after(acc, out5))
    acc = contract_slots([[(q6, x5), (b5, x5)]], ts, table, base6, q, w, acc)

    part = acc.sum((2, 3, 4)).reshape(2, structures, 2)
    total = part[0] + swap_cores(part[1])
    return sum((lax.ppermute(total, "ev", [(j, (j + k) % evs) for j in range(evs)]) for k in range(1, evs)), total)


def body(relay, *args):
    totals = (body_relay if relay else body_any)(*args)
    return (totals * float(args[0].shape[3]) ** -1.5)[None]


def solution(mesh):
    relay = mesh.shape["ev"] == 4 and mesh.shape["src"] == 4 and mesh.shape["grp"] == 2
    in_specs = (
        P("grp", "ev", None, None),
        P("src", None, None, "ev", None),
        P("src", None, None, "ev", None),
        P(),
        P(),
    )
    out_specs = P("src", "grp", None)
    return jax.shard_map(functools.partial(body, relay), mesh=mesh, in_specs=in_specs, out_specs=out_specs, check_vma=False)
```

```python
import functools

import jax
import jax.numpy as jnp
import numpy as np
from jax import lax
from jax.experimental import pallas as pl
from jax.experimental.pallas import tpu as pltpu
from jax.sharding import PartitionSpec as P

BF16, F32 = jnp.bfloat16, jnp.float32
LANES = 128
BLOCK = 8
STATED = 0.6


def project_kernel(at_ref, left_ref, source_ref, *refs):
    out_ref, near_ref, wide_ref = refs[-3:]
    structures, _, halves, per, rows, lanes = out_ref.shape
    parts, n = source_ref.shape[:2]
    for part in range(parts):
        for h in range(halves):
            one = source_ref[part, :, :, h * lanes : (h + 1) * lanes]
            wide_ref[part, h] = one.astype(F32).reshape(n * per, lanes)
    for i in range(per):
        one = [
            jnp.concatenate([wide_ref[part, h, pl.ds(i, n, stride=per), :].astype(BF16) for h in range(halves)], 1)
            for part in range(parts)
        ]
        got = jnp.dot(left_ref[...], jnp.concatenate(one, 0), preferred_element_type=F32)
        for h in range(halves):
            out_ref[:, :, h, i] = got[:, h * lanes : (h + 1) * lanes].reshape(structures, 2, rows, lanes)
    block = out_ref[:, :, :, :, pl.ds(pl.multiple_of(at_ref[0] * BLOCK, BLOCK), BLOCK), :]
    near_ref[0] = block.reshape(structures, 2, halves, per * BLOCK, lanes).astype(BF16)


def project_source(left, source, structures, block, near, place):
    parts, _, e, n = source.shape
    rows = left.shape[0] // (2 * structures)
    halves = n // LANES
    per = min(16, e)
    near_block = (1, structures, 2, halves, per * BLOCK, LANES)
    return pl.pallas_call(
        project_kernel,
        grid_spec=pltpu.PrefetchScalarGridSpec(
            num_scalar_prefetch=1,
            grid=(e // per,),
            in_specs=[
                pl.BlockSpec(left.shape, lambda i, at: (0, 0)),
                pl.BlockSpec((parts, n, per, n), lambda i, at: (0, 0, i, 0)),
            ]
            + ([] if near is None else [pl.BlockSpec(memory_space=pl.ANY)]),
            out_specs=[
                pl.BlockSpec((structures, 2, halves, per, rows, LANES), lambda i, at: (0, 0, 0, i, 0, 0)),
                pl.BlockSpec(near_block, lambda i, at: (place, 0, 0, 0, i, 0)),
            ],
            scratch_shapes=[pltpu.VMEM((parts, halves, n * per, LANES), F32)],
        ),
        out_shape=[
            jax.ShapeDtypeStruct((structures, 2, halves, e, rows, LANES), F32),
            jax.ShapeDtypeStruct((2, structures, 2, halves, e * BLOCK, LANES), BF16),
        ],
        input_output_aliases={} if near is None else {3: 1},
        compiler_params=pltpu.CompilerParams(vmem_limit_bytes=49 * 1024 * 1024),
        cost_estimate=pl.CostEstimate(
            flops=int(STATED * 2 * left.shape[0] * 2 * n * n * e),
            bytes_accessed=int(STATED * (2 * source.size + 4 * left.shape[0] * e * n)),
            transcendentals=0,
        ),
        name="project_source",
    )(scalars(block), left, source, *([] if near is None else [near]))


def contract_block(sink, t_views, q_ref, w_ref, out_ref, e):
    _, block, n, _ = sink.shape
    combos, _, halves, _, lanes = out_ref.shape
    structures = combos // len(t_views)
    group = block // 2
    for g, t_rows in enumerate(t_views):
        for s in range(structures):
            c = g * structures + s
            acc = [[jnp.zeros((8, lanes), F32) for _ in range(halves)] for _ in range(2)]
            for start in range(0, block, group):
                rows = [sink[part, start : start + group].reshape(group * n, n) for part in range(2)]
                first = jnp.dot(jnp.concatenate(rows, 1), w_ref[c], preferred_element_type=F32)
                first = first.astype(BF16)
                for a in range(group):
                    one = first[a * n : (a + 1) * n]
                    one = jnp.concatenate([one[:, :n], one[:, n:]], 0)
                    second = jnp.dot(q_ref[c], one, preferred_element_type=F32)
                    second = second.astype(BF16).astype(F32)
                    for h in range(halves):
                        re = second[:e, h * lanes : (h + 1) * lanes]
                        im = second[e:, h * lanes : (h + 1) * lanes]
                        base = (s * 2 * halves + h) * e * block + start + a
                        tre = t_rows[pl.ds(base, e, stride=block), :]
                        tim = t_rows[pl.ds(base + halves * e * block, e, stride=block), :]
                        acc[0][h] += (re * tre - im * tim).reshape(e // 8, 8, lanes).sum(0)
                        acc[1][h] += (re * tim + im * tre).reshape(e // 8, 8, lanes).sum(0)
            for part in range(2):
                for h in range(halves):
                    out_ref[c, part, h] += acc[part][h]


def t_view(ref):
    structures, _, halves, e, block, lanes = ref.shape
    return ref.reshape(structures * 2 * halves * e * block, lanes)


def contract_kernel(at_ref, sink_ref, *refs, sources, base):
    t_refs, (q_ref, w_ref, acc_ref, out_ref) = refs[:sources], refs[sources:]
    e = t_refs[0].shape[3]

    @pl.when(pl.program_id(0) == 0)
    def _():
        out_ref[...] = acc_ref[...]

    @pl.when(at_ref[base + 2] > 0)
    def _():
        contract_block(sink_ref, [t_view(t) for t in t_refs], q_ref, w_ref, out_ref, e)


def whole(ref):
    return pl.BlockSpec(ref.shape, lambda i, at: (0,) * ref.ndim)


def t_specs(ts, block_at):
    structures, _, halves, e, _, lanes = ts[0].shape
    shape = (structures, 2, halves, e, BLOCK, lanes)
    return [pl.BlockSpec(shape, lambda i, at: (0, 0, 0, 0, block_at(i, at), 0))] * len(ts)


def contract_cost(blocks, combos, n, e):
    blocks = STATED * blocks
    return pl.CostEstimate(
        flops=int(blocks * BLOCK * combos * 2 * (n * 2 * n * 2 * n + 2 * e * 2 * n * n)),
        bytes_accessed=int(blocks * BLOCK * (4 * n * n + combos * 8 * e * n)),
        transcendentals=0,
    )


def scalars(*values):
    return jnp.stack([jnp.asarray(v, jnp.int32) for v in values])


def contract(sink, ts, table, base, q, w, acc, blocks):
    n = sink.shape[2]
    return pl.pallas_call(
        functools.partial(contract_kernel, sources=len(ts), base=base),
        grid_spec=pltpu.PrefetchScalarGridSpec(
            num_scalar_prefetch=1,
            grid=(blocks,),
            in_specs=[pl.BlockSpec((2, BLOCK, n, n), lambda i, at: (0, at[base] + i, 0, 0))]
            + t_specs(ts, lambda i, at: at[base + 1] + i)
            + [whole(q), whole(w), whole(acc)],
            out_specs=whole(acc),
        ),
        out_shape=jax.ShapeDtypeStruct(acc.shape, F32),
        compiler_params=pltpu.CompilerParams(vmem_limit_bytes=49 * 1024 * 1024),
        cost_estimate=contract_cost(blocks, w.shape[0], n, ts[0].shape[3]),
        name="contract",
    )(table, sink, *ts, q, w, acc)


def slots_kernel(at_ref, *refs, sources, shapes, base):
    arrays = sum(len(parts) for choices in shapes for parts in choices)
    sinks, refs = refs[:arrays], refs[arrays:]
    t_refs, (q_ref, w_ref, acc_ref, out_ref, held, sem) = refs[:sources], refs[sources:]
    e = t_refs[0].shape[3]
    i = pl.program_id(0)

    def fetch(slot):
        place = sum(len(parts) for choices in shapes[:slot] for parts in choices)
        for k, parts in enumerate(shapes[slot]):

            @pl.when(at_ref[base + 2 * slot] == k + 1)
            def _():
                row = 0
                for part, size in enumerate(parts):
                    to = held.at[slot % 2, :, pl.ds(row, size)]
                    pltpu.make_async_copy(sinks[place + part], to, sem.at[slot % 2]).start()
                    row += size

            place += len(parts)

    @pl.when(i == 0)
    def _():
        fetch(0)
        out_ref[...] = acc_ref[...]

    for slot in range(1, len(shapes)):

        @pl.when(i == slot - 1)
        def _():
            fetch(slot)

    @pl.when(at_ref[base + 2 * i] > 0)
    def _():
        now = lax.rem(i, 2)
        pltpu.make_async_copy(held.at[now], held.at[now], sem.at[now]).wait()
        contract_block(held.at[now], [t_view(t) for t in t_refs], q_ref, w_ref, out_ref, e)


def contract_slots(slots, ts, table, base, q, w, acc):
    n = q.shape[2] // 2
    arrays = [part for choices in slots for parts in choices for part in parts]
    shapes = tuple(tuple(tuple(part.shape[1] for part in parts) for parts in choices) for choices in slots)
    return pl.pallas_call(
        functools.partial(slots_kernel, sources=len(ts), shapes=shapes, base=base),
        grid_spec=pltpu.PrefetchScalarGridSpec(
            num_scalar_prefetch=1,
            grid=(len(slots),),
            in_specs=[pl.BlockSpec(memory_space=pl.ANY)] * len(arrays)
            + t_specs(ts, lambda i, at: at[base + 2 * i + 1])
            + [whole(q), whole(w), whole(acc)],
            out_specs=whole(acc),
            scratch_shapes=[pltpu.VMEM((2, 2, BLOCK, n, n), BF16), pltpu.SemaphoreType.DMA((2,))],
        ),
        out_shape=jax.ShapeDtypeStruct(acc.shape, F32),
        compiler_params=pltpu.CompilerParams(vmem_limit_bytes=49 * 1024 * 1024),
        cost_estimate=contract_cost(len(slots), w.shape[0], n, ts[0].shape[3]),
        name="contract_slots",
    )(table, *arrays, *ts, q, w, acc)


def near_kernel(at_ref, sink_ref, t_ref, other_ref, q_ref, w_ref, acc_ref, out_ref, wide_ref, *, base):
    e = q_ref.shape[1] // 2
    i = pl.program_id(0)

    @pl.when(i == 0)
    def _():
        out_ref[...] = acc_ref[...]

    @pl.when(at_ref[base + 2] > 0)
    def _():
        sources = t_ref.shape[0]

        @pl.when(i == 0)
        def _():
            wide_ref[...] = t_ref[...].reshape(wide_ref.shape).astype(F32)

        @pl.when(i == 1)
        def _():
            wide_ref[...] = other_ref[...].reshape(wide_ref.shape).astype(F32)

        contract_block(sink_ref, [wide_ref.at[g] for g in range(sources)], q_ref, w_ref, out_ref, e)


def contract_near(sink, t, other, table, base, q, w, acc):
    n = sink.shape[2]
    return pl.pallas_call(
        functools.partial(near_kernel, base=base),
        grid_spec=pltpu.PrefetchScalarGridSpec(
            num_scalar_prefetch=1,
            grid=(2,),
            in_specs=[pl.BlockSpec((2, BLOCK, n, n), lambda i, at: (0, at[base + i], 0, 0))]
            + [whole(t), whole(other), whole(q), whole(w), whole(acc)],
            out_specs=whole(acc),
            scratch_shapes=[pltpu.VMEM((t.shape[0], t.size // t.shape[0] // LANES, LANES), F32)],
        ),
        out_shape=jax.ShapeDtypeStruct(acc.shape, F32),
        compiler_params=pltpu.CompilerParams(vmem_limit_bytes=49 * 1024 * 1024),
        cost_estimate=contract_cost(2, w.shape[0], n, q.shape[1] // 2),
        name="contract_near",
    )(table, sink, t, other, q, w, acc)


def after(value, *others):
    return lax.optimization_barrier((value, *others))[0]


def rows_to_send(perambulators, source_times):
    position, srcs = lax.axis_index("src"), lax.axis_size("src")
    held = perambulators.shape[0]
    out = []
    for k in range(1, srcs):
        to = lax.rem(position + srcs - k, srcs)
        within = lax.dynamic_index_in_dim(source_times, to, 0, keepdims=False) - position * held
        out.append(lax.dynamic_index_in_dim(perambulators, jnp.clip(within, 0, held - 1), 0, keepdims=False))
    return out


def own_rows(sent, held, source_times):
    position, srcs = lax.axis_index("src"), lax.axis_size("src")
    own_time = lax.dynamic_index_in_dim(source_times, position, 0, keepdims=False)
    chosen = None
    for k in range(1, srcs):
        got = lax.ppermute(sent[k - 1], "src", [(j, (j + srcs - k) % srcs) for j in range(srcs)])
        here = own_time // held == lax.rem(position + k, srcs)
        chosen = got if chosen is None else jnp.where(here, got, chosen)
    return chosen


def all_rows(rows):
    return lax.all_gather(rows, "ev", axis=2, tiled=True)


def maps_kernel(at_ref, *refs, sources, chunks, stride, e):
    times, left_refs, (right_ref, *middle_refs, turned) = refs[:sources], refs[sources : 2 * sources], refs[2 * sources :]
    _, parts, n, _ = times[0].shape
    structures = right_ref.shape[0] // sources
    size = left_refs[0].shape[0] // (structures * 2 * chunks)
    start = at_ref[3 * structures]
    for g in range(sources):
        for s in range(structures):
            first, second, third = (times[g].at[at_ref[3 * s + k]] for k in range(3))
            for k in range(chunks):
                rows = pl.ds(pl.multiple_of(start + k * stride, size), size)
                re, im = first[0, rows, :], first[1, rows, :]
                for part, (x, y) in enumerate(((re, im), (im, -re))):
                    to = ((s * 2 + part) * chunks + k) * size
                    left_refs[g][to : to + size, :n] = x
                    left_refs[g][to : to + size, n:] = y
            c = g * structures + s
            re, im = third[0], third[1]
            right_ref[c, :n, :n] = re
            right_ref[c, :n, n:] = im
            right_ref[c, n:, :n] = -im
            right_ref[c, n:, n:] = re
            for part in range(parts):
                turned[part] = second[part].astype(F32).T
            for k, middle_ref in enumerate(middle_refs):
                columns = pl.ds(pl.multiple_of(at_ref[3 * structures + 1 + k], e), e)
                re, im = turned[0, columns, :], turned[1, columns, :]
                middle_ref[c, :, :n] = jnp.concatenate([re, im], 0).astype(BF16)
                middle_ref[c, :, n:] = jnp.concatenate([-im, re], 0).astype(BF16)


def maps(times, spin_index, first_row, chunks, size, stride, e, places):
    n = times[0].shape[2]
    structures, sources = spin_index.shape[0], len(times)
    combos = sources * structures
    at = jnp.concatenate([spin_index.reshape(-1), scalars(first_row, *places)])
    shapes = [(structures * 2 * chunks * size, 2 * n)] * sources + [(combos, 2 * n, 2 * n)] + [(combos, 2 * e, 2 * n)] * len(places)
    return pl.pallas_call(
        functools.partial(maps_kernel, sources=sources, chunks=chunks, stride=stride, e=e),
        grid_spec=pltpu.PrefetchScalarGridSpec(
            num_scalar_prefetch=1,
            grid=(1,),
            in_specs=[whole(t) for t in times],
            out_specs=[pl.BlockSpec(shape, lambda i, at, d=len(shape): (0,) * d) for shape in shapes],
            scratch_shapes=[pltpu.VMEM((2, n, n), F32)],
        ),
        out_shape=[jax.ShapeDtypeStruct(shape, BF16) for shape in shapes],
        compiler_params=pltpu.CompilerParams(vmem_limit_bytes=48 * 1024 * 1024),
        name="maps",
    )(at, *times)


def body_any(sink_tensor, source_tensor, perambulators, source_times, spin_index):
    position, ev = lax.axis_index("src"), lax.axis_index("ev")
    evs, srcs = lax.axis_size("ev"), lax.axis_size("src")
    structures = spin_index.shape[0]
    _, slice_a, n, _ = sink_tensor.shape
    e = n // evs
    share = slice_a // srcs
    mine = lax.dynamic_slice_in_dim(sink_tensor, position * share, share, axis=1)
    sink = lax.all_gather(mine, ("ev", "src"), axis=1, tiled=True)
    sent = rows_to_send(perambulators, source_times)
    per_time = all_rows(own_rows(sent, perambulators.shape[0], source_times))
    left, w, q = maps([per_time], spin_index, 0, 1, n, n, e, [ev * e])
    t, _ = project_source(left, source_tensor[0], structures, 0, None, 0)
    acc = jnp.zeros((structures, 2, n // LANES, 8, LANES), F32)
    acc = contract(sink, [t], scalars(0, 0, 1), 0, q, w, acc, n // BLOCK)
    return lax.psum(acc.sum((2, 3, 4)), "ev")


RELAY_CALLS = (
    (
        (("near", "u0"), None, 1),
        (None, ("opposite", "u0"), 1),
        (("near", "p0"), ("opposite", "p0"), 1),
    ),
    (
        (("across", "u0"), ("near", "u0"), 2),
        (None, ("opposite", "u1"), 1),
    ),
    (
        (("across", "p0"), ("near", "p0"), 1),
        (("across", "u1"), ("near", "u1"), 2),
    ),
    (
        (("opposite", "u0"), ("across", "u0"), 2),
        (("across", "p1"), ("opposite", "p1"), 1),
        (None, ("near", "u2"), 1),
    ),
    (
        (("opposite", "p0"), ("across", "p0"), 1),
        (("opposite", "u1"), ("across", "u1"), 2),
    ),
    ((("opposite", "p1"), ("across", "p1"), 2),),
)
OWN_TABLE = 12
BASES = tuple(OWN_TABLE + 2 * sum(len(call) for call in RELAY_CALLS[:k]) for k in range(len(RELAY_CALLS)))


def relay_table(evs, units):
    rows = []
    for ev in range(evs):
        for position in range(4):
            for grp in range(2):
                chip, core = position // 2, position % 2
                end = int(ev in (0, evs - 1))
                near = 1 - ev if ev < 2 else 5 - ev
                slices = dict(near=near, opposite=3 - ev, across=3 - near)
                unit = {f"u{w}": units - 1 - w if chip else w for w in range(units)}
                unit |= {f"p{w}": w if chip else units - 1 - w for w in range(units)}
                row = [core * units, ev * units, 1]
                row += [core * units + 1, ev * units + 1, 1]
                row += [core * units + units // 2, ev * units + units // 2, 1]
                row += [core * units + 1 + grp, core * units + 2 - grp, 1 - end]
                for call in RELAY_CALLS:
                    for at_end, at_inner, choices in call:
                        at = at_end if end else at_inner
                        which = 0 if at is None else 1 if end or choices == 1 else 2
                        row += [which, 0 if at is None else slices[at[0]] * units + unit[at[1]]]
                rows.append(row)
    return np.array(rows, np.int32)


def body_relay(sink_tensor, source_tensor, perambulators, source_times, spin_index):
    position, ev, grp = lax.axis_index("src"), lax.axis_index("ev"), lax.axis_index("grp")
    evs, srcs = lax.axis_size("ev"), lax.axis_size("src")
    structures = spin_index.shape[0]
    _, slice_a, n, _ = sink_tensor.shape
    e = n // evs
    chip, core = position // 2, position % 2
    half = slice_a // 2
    units = half // BLOCK
    is_end = (ev == 0) | (ev == evs - 1)
    near = jnp.where(ev < 2, 1 - ev, 5 - ev)

    def unit(w):
        return jnp.where(chip == 0, w, units - 1 - w)

    def own(w, start=0, size=BLOCK):
        return lax.dynamic_slice_in_dim(sink_tensor, core * half + BLOCK * unit(w) + start, size, axis=1)

    outward = lambda v: lax.ppermute(v, "ev", [(1, 0), (2, 3)])
    inward = lambda v: lax.ppermute(v, "ev", [(0, 1), (3, 2)])
    middle = lambda v: lax.ppermute(v, "ev", [(1, 2), (2, 1)])
    swap_chips = lambda v: lax.ppermute(v, "src", [(0, 2), (2, 0), (1, 3), (3, 1)])
    swap_cores = lambda v: lax.ppermute(v, "src", [(0, 1), (1, 0), (2, 3), (3, 2)])
    swap_groups = lambda v: lax.ppermute(v, "grp", [(0, 1), (1, 0)])

    table = jnp.asarray(relay_table(evs, units))
    table = lax.dynamic_index_in_dim(table, (ev * 4 + position) * 2 + grp, 0, keepdims=False)
    base1, base2, base3, base4, base5, base6 = BASES

    choose = lambda a, b: jnp.where(is_end, a, b)

    sent = rows_to_send(perambulators, source_times)
    rows_here = own_rows(sent, perambulators.shape[0], source_times)
    spins = rows_here.shape[0]
    own0 = own(0)
    rows_here = after(rows_here, own0, table)
    some = lax.dynamic_slice_in_dim(rows_here, grp * (spins // 2), spins // 2, axis=0)
    mine = jnp.stack([lax.ppermute(some, "ev", [(j, (j + k) % evs) for j in range(evs)]) for k in range(1, evs)])
    own1, own2a, own2b = own(1), own(2, 0, BLOCK // 2), own(2, BLOCK // 2, BLOCK // 2)
    others = swap_groups(after(mine, own1, own2a, own2b))
    whole_rows = jnp.where(grp == 0, jnp.concatenate([mine, others], 1), jnp.concatenate([others, mine], 1))
    whole_rows = [rows_here if k == 0 else whole_rows[k - 1] for k in range(evs)]
    turned = jnp.stack([whole_rows[(evs - 1 - k) % evs] for k in range(2 * evs - 1)])
    turned = lax.dynamic_slice_in_dim(turned, evs - 1 - ev, evs, axis=0)
    per_time = turned.transpose(1, 2, 0, 3, 4).reshape(spins, 2, n, n)
    other_time = swap_cores(per_time)
    source = source_tensor[0]
    other_source = swap_cores(after(source, rows_here))
    *lefts, w, q, q_near = maps(
        [per_time, other_time], spin_index, core * half, evs, half, slice_a, e, [ev * e, near * e]
    )
    own0, own1 = after((own0, own1), mine)
    b1, q1, e2, b3 = middle(own0), outward(own0), inward(own0), middle(own1)
    acc = jnp.zeros((2 * structures, 2, n // LANES, 8, LANES), F32)

    block = near * units + 1 + grp
    t_own, to_near = project_source(lefts[0], source, structures, block, None, 0)
    b1, q1 = after((b1, q1), t_own)
    q2 = outward(b1)
    out1 = choose(q1, b1)
    x1 = swap_chips(out1)
    e3, e1a, e1b = inward(after(own1, out1)), inward(after(own2a, out1)), inward(after(own2b, out1))
    t_other, to_near = project_source(lefts[1], after(other_source, t_own, b1, q1, out1), structures, block, to_near, 1)
    ts = (t_own, t_other)
    b2 = middle(after(e2, t_other))
    near_t = inward(after(to_near, t_other))
    acc = contract(sink_tensor, ts, table, 0, q, w, after(acc, e2), 1)
    q3 = outward(after(b3, acc))
    acc = contract(sink_tensor, ts, table, 3, q, w, after(acc, b3), 1)
    out2 = choose(after(q2, acc), e2)
    x2 = swap_chips(out2)
    acc = contract(sink_tensor, ts, table, 6, q, w, after(acc, out2, x1), units // 2)
    acc = contract_slots([[(q1,)], [(b1,)], [(x1,)]], ts, table, base1, q, w, acc)
    q4 = outward(after(b2, acc))
    b4 = middle(after(e3, acc))
    out3 = choose(after(q3, acc), b3)
    x3 = swap_chips(out3)
    far_t = swap_groups(after(near_t, acc))
    acc = contract_slots([[(q2,), (e2,)], [(b3,)]], ts, table, base2, q, w, after(acc, b2, e3, out3, near_t))
    b5 = middle(after(e1a, acc))
    acc = contract_slots([[(x2,)], [(q3,), (e3,)]], ts, table, base3, q, w, after(acc, e1a))
    q5 = outward(after(b4, acc))
    out4 = choose(after(q4, acc), b2)
    x4 = swap_chips(out4)
    acc = contract_slots([[(q4,), (b2,)], [(x3,)], [(e1a, e1b)]], ts, table, base4, q, w, after(acc, b4, out4))
    q6 = outward(after(b5, acc))
    acc = contract_near(sink_tensor, near_t, far_t, table, 9, q_near, w, after(acc, b5))
    out5 = choose(after(q5, acc), b4)[:, BLOCK // 2 :]
    x5 = swap_chips(out5)
    acc = contract_slots([[(x4,)], [(q5,), (b4,)]], ts, table, base5, q, w, after(acc, out5))
    acc = contract_slots([[(q6, x5), (b5, x5)]], ts, table, base6, q, w, acc)

    part = acc.sum((2, 3, 4)).reshape(2, structures, 2)
    total = part[0] + swap_cores(part[1])
    return sum((lax.ppermute(total, "ev", [(j, (j + k) % evs) for j in range(evs)]) for k in range(1, evs)), total)


def body(relay, *args):
    totals = (body_relay if relay else body_any)(*args)
    return (totals * float(args[0].shape[3]) ** -1.5)[None]


def solution(mesh):
    relay = mesh.shape["ev"] == 4 and mesh.shape["src"] == 4 and mesh.shape["grp"] == 2
    in_specs = (
        P("grp", "ev", None, None),
        P("src", None, None, "ev", None),
        P("src", None, None, "ev", None),
        P(),
        P(),
    )
    out_specs = P("src", "grp", None)
    return jax.shard_map(functools.partial(body, relay), mesh=mesh, in_specs=in_specs, out_specs=out_specs, check_vma=False)
```

```python
import functools

import jax
import jax.numpy as jnp
import numpy as np
from jax import lax
from jax.experimental import pallas as pl
from jax.experimental.pallas import tpu as pltpu
from jax.sharding import PartitionSpec as P

BF16, F32 = jnp.bfloat16, jnp.float32
LANES = 128
BLOCK = 8
STATED = 0.6


def project_kernel(at_ref, left_ref, source_ref, *refs):
    out_ref, near_ref, wide_ref = refs[-3:]
    structures, _, halves, per, rows, lanes = out_ref.shape
    parts, n = source_ref.shape[:2]
    for part in range(parts):
        for h in range(halves):
            one = source_ref[part, :, :, h * lanes : (h + 1) * lanes]
            wide_ref[part, h] = one.astype(F32).reshape(n * per, lanes)
    for i in range(per):
        one = [
            jnp.concatenate([wide_ref[part, h, pl.ds(i, n, stride=per), :].astype(BF16) for h in range(halves)], 1)
            for part in range(parts)
        ]
        got = jnp.dot(left_ref[...], jnp.concatenate(one, 0), preferred_element_type=F32)
        for h in range(halves):
            out_ref[:, :, h, i] = got[:, h * lanes : (h + 1) * lanes].reshape(structures, 2, rows, lanes)
    block = out_ref[:, :, :, :, pl.ds(pl.multiple_of(at_ref[0] * BLOCK, BLOCK), BLOCK), :]
    near_ref[0] = block.reshape(structures, 2, halves, per * BLOCK, lanes).astype(BF16)


def project_source(left, source, structures, block, near, place):
    parts, _, e, n = source.shape
    rows = left.shape[0] // (2 * structures)
    halves = n // LANES
    per = min(16, e)
    near_block = (1, structures, 2, halves, per * BLOCK, LANES)
    return pl.pallas_call(
        project_kernel,
        grid_spec=pltpu.PrefetchScalarGridSpec(
            num_scalar_prefetch=1,
            grid=(e // per,),
            in_specs=[
                pl.BlockSpec(left.shape, lambda i, at: (0, 0)),
                pl.BlockSpec((parts, n, per, n), lambda i, at: (0, 0, i, 0)),
            ]
            + ([] if near is None else [pl.BlockSpec(memory_space=pl.ANY)]),
            out_specs=[
                pl.BlockSpec((structures, 2, halves, per, rows, LANES), lambda i, at: (0, 0, 0, i, 0, 0)),
                pl.BlockSpec(near_block, lambda i, at: (place, 0, 0, 0, i, 0)),
            ],
            scratch_shapes=[pltpu.VMEM((parts, halves, n * per, LANES), F32)],
        ),
        out_shape=[
            jax.ShapeDtypeStruct((structures, 2, halves, e, rows, LANES), F32),
            jax.ShapeDtypeStruct((2, structures, 2, halves, e * BLOCK, LANES), BF16),
        ],
        input_output_aliases={} if near is None else {3: 1},
        compiler_params=pltpu.CompilerParams(vmem_limit_bytes=49 * 1024 * 1024),
        cost_estimate=pl.CostEstimate(
            flops=int(STATED * 2 * left.shape[0] * 2 * n * n * e),
            bytes_accessed=int(STATED * (2 * source.size + 4 * left.shape[0] * e * n)),
            transcendentals=0,
        ),
        name="project_source",
    )(scalars(block), left, source, *([] if near is None else [near]))


def contract_block(sink, t_views, q_ref, w_ref, out_ref, e):
    _, block, n, _ = sink.shape
    combos, _, halves, _, lanes = out_ref.shape
    structures = combos // len(t_views)
    group = block // 2
    for g, t_rows in enumerate(t_views):
        for s in range(structures):
            c = g * structures + s
            acc = [[jnp.zeros((8, lanes), F32) for _ in range(halves)] for _ in range(2)]
            for start in range(0, block, group):
                rows = [sink[part, start : start + group].reshape(group * n, n) for part in range(2)]
                first = jnp.dot(jnp.concatenate(rows, 1), w_ref[c], preferred_element_type=F32)
                first = first.astype(BF16)
                for a in range(group):
                    one = first[a * n : (a + 1) * n]
                    one = jnp.concatenate([one[:, :n], one[:, n:]], 0)
                    second = jnp.dot(q_ref[c], one, preferred_element_type=F32)
                    second = second.astype(BF16).astype(F32)
                    for h in range(halves):
                        re = second[:e, h * lanes : (h + 1) * lanes]
                        im = second[e:, h * lanes : (h + 1) * lanes]
                        base = (s * 2 * halves + h) * e * block + start + a
                        tre = t_rows[pl.ds(base, e, stride=block), :]
                        tim = t_rows[pl.ds(base + halves * e * block, e, stride=block), :]
                        acc[0][h] += (re * tre - im * tim).reshape(e // 8, 8, lanes).sum(0)
                        acc[1][h] += (re * tim + im * tre).reshape(e // 8, 8, lanes).sum(0)
            for part in range(2):
                for h in range(halves):
                    out_ref[c, part, h] += acc[part][h]


def t_view(ref):
    structures, _, halves, e, block, lanes = ref.shape
    return ref.reshape(structures * 2 * halves * e * block, lanes)


def contract_kernel(at_ref, sink_ref, *refs, sources, base):
    t_refs, (q_ref, w_ref, acc_ref, out_ref) = refs[:sources], refs[sources:]
    e = t_refs[0].shape[3]

    @pl.when(pl.program_id(0) == 0)
    def _():
        out_ref[...] = acc_ref[...]

    @pl.when(at_ref[base + 2] > 0)
    def _():
        contract_block(sink_ref, [t_view(t) for t in t_refs], q_ref, w_ref, out_ref, e)


def whole(ref):
    return pl.BlockSpec(ref.shape, lambda i, at: (0,) * ref.ndim)


def t_specs(ts, block_at):
    structures, _, halves, e, _, lanes = ts[0].shape
    shape = (structures, 2, halves, e, BLOCK, lanes)
    return [pl.BlockSpec(shape, lambda i, at: (0, 0, 0, 0, block_at(i, at), 0))] * len(ts)


def contract_cost(blocks, combos, n, e):
    blocks = STATED * blocks
    return pl.CostEstimate(
        flops=int(blocks * BLOCK * combos * 2 * (n * 2 * n * 2 * n + 2 * e * 2 * n * n)),
        bytes_accessed=int(blocks * BLOCK * (4 * n * n + combos * 8 * e * n)),
        transcendentals=0,
    )


def scalars(*values):
    return jnp.stack([jnp.asarray(v, jnp.int32) for v in values])


def contract(sink, ts, table, base, q, w, acc, blocks):
    n = sink.shape[2]
    return pl.pallas_call(
        functools.partial(contract_kernel, sources=len(ts), base=base),
        grid_spec=pltpu.PrefetchScalarGridSpec(
            num_scalar_prefetch=1,
            grid=(blocks,),
            in_specs=[pl.BlockSpec((2, BLOCK, n, n), lambda i, at: (0, at[base] + i, 0, 0))]
            + t_specs(ts, lambda i, at: at[base + 1] + i)
            + [whole(q), whole(w), whole(acc)],
            out_specs=whole(acc),
        ),
        out_shape=jax.ShapeDtypeStruct(acc.shape, F32),
        compiler_params=pltpu.CompilerParams(vmem_limit_bytes=49 * 1024 * 1024),
        cost_estimate=contract_cost(blocks, w.shape[0], n, ts[0].shape[3]),
        name="contract",
    )(table, sink, *ts, q, w, acc)


def slots_kernel(at_ref, *refs, sources, shapes, base):
    arrays = sum(len(parts) for choices in shapes for parts in choices)
    sinks, refs = refs[:arrays], refs[arrays:]
    t_refs, (q_ref, w_ref, acc_ref, out_ref, held, sem) = refs[:sources], refs[sources:]
    e = t_refs[0].shape[3]
    i = pl.program_id(0)

    def fetch(slot):
        place = sum(len(parts) for choices in shapes[:slot] for parts in choices)
        for k, parts in enumerate(shapes[slot]):

            @pl.when(at_ref[base + 2 * slot] == k + 1)
            def _():
                row = 0
                for part, size in enumerate(parts):
                    to = held.at[slot % 2, :, pl.ds(row, size)]
                    pltpu.make_async_copy(sinks[place + part], to, sem.at[slot % 2]).start()
                    row += size

            place += len(parts)

    @pl.when(i == 0)
    def _():
        fetch(0)
        out_ref[...] = acc_ref[...]

    for slot in range(1, len(shapes)):

        @pl.when(i == slot - 1)
        def _():
            fetch(slot)

    @pl.when(at_ref[base + 2 * i] > 0)
    def _():
        now = lax.rem(i, 2)
        pltpu.make_async_copy(held.at[now], held.at[now], sem.at[now]).wait()
        contract_block(held.at[now], [t_view(t) for t in t_refs], q_ref, w_ref, out_ref, e)


def contract_slots(slots, ts, table, base, q, w, acc):
    n = q.shape[2] // 2
    arrays = [part for choices in slots for parts in choices for part in parts]
    shapes = tuple(tuple(tuple(part.shape[1] for part in parts) for parts in choices) for choices in slots)
    return pl.pallas_call(
        functools.partial(slots_kernel, sources=len(ts), shapes=shapes, base=base),
        grid_spec=pltpu.PrefetchScalarGridSpec(
            num_scalar_prefetch=1,
            grid=(len(slots),),
            in_specs=[pl.BlockSpec(memory_space=pl.ANY)] * len(arrays)
            + t_specs(ts, lambda i, at: at[base + 2 * i + 1])
            + [whole(q), whole(w), whole(acc)],
            out_specs=whole(acc),
            scratch_shapes=[pltpu.VMEM((2, 2, BLOCK, n, n), BF16), pltpu.SemaphoreType.DMA((2,))],
        ),
        out_shape=jax.ShapeDtypeStruct(acc.shape, F32),
        compiler_params=pltpu.CompilerParams(vmem_limit_bytes=49 * 1024 * 1024),
        cost_estimate=contract_cost(len(slots), w.shape[0], n, ts[0].shape[3]),
        name="contract_slots",
    )(table, *arrays, *ts, q, w, acc)


def near_kernel(at_ref, sink_ref, t_ref, other_ref, q_ref, w_ref, acc_ref, out_ref, wide_ref, *, base):
    e = q_ref.shape[1] // 2
    i = pl.program_id(0)

    @pl.when(i == 0)
    def _():
        out_ref[...] = acc_ref[...]

    @pl.when(at_ref[base + 2] > 0)
    def _():
        sources = t_ref.shape[0]

        @pl.when(i == 0)
        def _():
            wide_ref[...] = t_ref[...].reshape(wide_ref.shape).astype(F32)

        @pl.when(i == 1)
        def _():
            wide_ref[...] = other_ref[...].reshape(wide_ref.shape).astype(F32)

        contract_block(sink_ref, [wide_ref.at[g] for g in range(sources)], q_ref, w_ref, out_ref, e)


def contract_near(sink, t, other, table, base, q, w, acc):
    n = sink.shape[2]
    return pl.pallas_call(
        functools.partial(near_kernel, base=base),
        grid_spec=pltpu.PrefetchScalarGridSpec(
            num_scalar_prefetch=1,
            grid=(2,),
            in_specs=[pl.BlockSpec((2, BLOCK, n, n), lambda i, at: (0, at[base + i], 0, 0))]
            + [whole(t), whole(other), whole(q), whole(w), whole(acc)],
            out_specs=whole(acc),
            scratch_shapes=[pltpu.VMEM((t.shape[0], t.size // t.shape[0] // LANES, LANES), F32)],
        ),
        out_shape=jax.ShapeDtypeStruct(acc.shape, F32),
        compiler_params=pltpu.CompilerParams(vmem_limit_bytes=49 * 1024 * 1024),
        cost_estimate=contract_cost(2, w.shape[0], n, q.shape[1] // 2),
        name="contract_near",
    )(table, sink, t, other, q, w, acc)


def after(value, *others):
    return lax.optimization_barrier((value, *others))[0]


def rows_to_send(perambulators, source_times):
    position, srcs = lax.axis_index("src"), lax.axis_size("src")
    held = perambulators.shape[0]
    out = []
    for k in range(1, srcs):
        to = lax.rem(position + srcs - k, srcs)
        within = lax.dynamic_index_in_dim(source_times, to, 0, keepdims=False) - position * held
        out.append(lax.dynamic_index_in_dim(perambulators, jnp.clip(within, 0, held - 1), 0, keepdims=False))
    return out


def own_rows(sent, held, source_times):
    position, srcs = lax.axis_index("src"), lax.axis_size("src")
    own_time = lax.dynamic_index_in_dim(source_times, position, 0, keepdims=False)
    chosen = None
    for k in range(1, srcs):
        got = lax.ppermute(sent[k - 1], "src", [(j, (j + srcs - k) % srcs) for j in range(srcs)])
        here = own_time // held == lax.rem(position + k, srcs)
        chosen = got if chosen is None else jnp.where(here, got, chosen)
    return chosen


def all_rows(rows):
    return lax.all_gather(rows, "ev", axis=2, tiled=True)


def maps_kernel(at_ref, *refs, sources, chunks, stride, e):
    times, left_refs, (right_ref, *middle_refs, turned) = refs[:sources], refs[sources : 2 * sources], refs[2 * sources :]
    _, parts, n, _ = times[0].shape
    structures = right_ref.shape[0] // sources
    size = left_refs[0].shape[0] // (structures * 2 * chunks)
    start = at_ref[3 * structures]
    for g in range(sources):
        for s in range(structures):
            first, second, third = (times[g].at[at_ref[3 * s + k]] for k in range(3))
            for k in range(chunks):
                rows = pl.ds(pl.multiple_of(start + k * stride, size), size)
                re, im = first[0, rows, :], first[1, rows, :]
                for part, (x, y) in enumerate(((re, im), (im, -re))):
                    to = ((s * 2 + part) * chunks + k) * size
                    left_refs[g][to : to + size, :n] = x
                    left_refs[g][to : to + size, n:] = y
            c = g * structures + s
            re, im = third[0], third[1]
            right_ref[c, :n, :n] = re
            right_ref[c, :n, n:] = im
            right_ref[c, n:, :n] = -im
            right_ref[c, n:, n:] = re
            for part in range(parts):
                turned[part] = second[part].astype(F32).T
            for k, middle_ref in enumerate(middle_refs):
                columns = pl.ds(pl.multiple_of(at_ref[3 * structures + 1 + k], e), e)
                re, im = turned[0, columns, :], turned[1, columns, :]
                middle_ref[c, :, :n] = jnp.concatenate([re, im], 0).astype(BF16)
                middle_ref[c, :, n:] = jnp.concatenate([-im, re], 0).astype(BF16)


def maps(times, spin_index, first_row, chunks, size, stride, e, places):
    n = times[0].shape[2]
    structures, sources = spin_index.shape[0], len(times)
    combos = sources * structures
    at = jnp.concatenate([spin_index.reshape(-1), scalars(first_row, *places)])
    shapes = [(structures * 2 * chunks * size, 2 * n)] * sources + [(combos, 2 * n, 2 * n)] + [(combos, 2 * e, 2 * n)] * len(places)
    return pl.pallas_call(
        functools.partial(maps_kernel, sources=sources, chunks=chunks, stride=stride, e=e),
        grid_spec=pltpu.PrefetchScalarGridSpec(
            num_scalar_prefetch=1,
            grid=(1,),
            in_specs=[whole(t) for t in times],
            out_specs=[pl.BlockSpec(shape, lambda i, at, d=len(shape): (0,) * d) for shape in shapes],
            scratch_shapes=[pltpu.VMEM((2, n, n), F32)],
        ),
        out_shape=[jax.ShapeDtypeStruct(shape, BF16) for shape in shapes],
        compiler_params=pltpu.CompilerParams(vmem_limit_bytes=48 * 1024 * 1024),
        name="maps",
    )(at, *times)


def body_any(sink_tensor, source_tensor, perambulators, source_times, spin_index):
    position, ev = lax.axis_index("src"), lax.axis_index("ev")
    evs, srcs = lax.axis_size("ev"), lax.axis_size("src")
    structures = spin_index.shape[0]
    _, slice_a, n, _ = sink_tensor.shape
    e = n // evs
    share = slice_a // srcs
    mine = lax.dynamic_slice_in_dim(sink_tensor, position * share, share, axis=1)
    sink = lax.all_gather(mine, ("ev", "src"), axis=1, tiled=True)
    sent = rows_to_send(perambulators, source_times)
    per_time = all_rows(own_rows(sent, perambulators.shape[0], source_times))
    left, w, q = maps([per_time], spin_index, 0, 1, n, n, e, [ev * e])
    t, _ = project_source(left, source_tensor[0], structures, 0, None, 0)
    acc = jnp.zeros((structures, 2, n // LANES, 8, LANES), F32)
    acc = contract(sink, [t], scalars(0, 0, 1), 0, q, w, acc, n // BLOCK)
    return lax.psum(acc.sum((2, 3, 4)), "ev")


RELAY_CALLS = (
    (
        (("near", "u0"), None, 1),
        (None, ("opposite", "u0"), 1),
        (("near", "p0"), ("opposite", "p0"), 1),
    ),
    (
        (("across", "u0"), ("near", "u0"), 2),
        (None, ("opposite", "u1"), 1),
    ),
    (
        (("across", "p0"), ("near", "p0"), 1),
        (("across", "u1"), ("near", "u1"), 2),
    ),
    (
        (("opposite", "u0"), ("across", "u0"), 2),
        (("across", "p1"), ("opposite", "p1"), 1),
        (None, ("near", "u2"), 1),
    ),
    (
        (("opposite", "p0"), ("across", "p0"), 1),
        (("opposite", "u1"), ("across", "u1"), 2),
    ),
    ((("opposite", "p1"), ("across", "p1"), 2),),
)
OWN_TABLE = 12
BASES = tuple(OWN_TABLE + 2 * sum(len(call) for call in RELAY_CALLS[:k]) for k in range(len(RELAY_CALLS)))


def relay_table(evs, units):
    rows = []
    for ev in range(evs):
        for position in range(4):
            for grp in range(2):
                chip, core = position // 2, position % 2
                end = int(ev in (0, evs - 1))
                near = 1 - ev if ev < 2 else 5 - ev
                slices = dict(near=near, opposite=3 - ev, across=3 - near)
                unit = {f"u{w}": units - 1 - w if chip else w for w in range(units)}
                unit |= {f"p{w}": w if chip else units - 1 - w for w in range(units)}
                row = [core * units, ev * units, 1]
                row += [core * units + 1, ev * units + 1, 1]
                row += [core * units + units // 2, ev * units + units // 2, 1]
                row += [core * units + 1 + grp, core * units + 2 - grp, 1 - end]
                for call in RELAY_CALLS:
                    for at_end, at_inner, choices in call:
                        at = at_end if end else at_inner
                        which = 0 if at is None else 1 if end or choices == 1 else 2
                        row += [which, 0 if at is None else slices[at[0]] * units + unit[at[1]]]
                rows.append(row)
    return np.array(rows, np.int32)


def body_relay(sink_tensor, source_tensor, perambulators, source_times, spin_index):
    position, ev, grp = lax.axis_index("src"), lax.axis_index("ev"), lax.axis_index("grp")
    evs, srcs = lax.axis_size("ev"), lax.axis_size("src")
    structures = spin_index.shape[0]
    _, slice_a, n, _ = sink_tensor.shape
    e = n // evs
    chip, core = position // 2, position % 2
    half = slice_a // 2
    units = half // BLOCK
    is_end = (ev == 0) | (ev == evs - 1)
    near = jnp.where(ev < 2, 1 - ev, 5 - ev)

    def unit(w):
        return jnp.where(chip == 0, w, units - 1 - w)

    def own(w, start=0, size=BLOCK):
        return lax.dynamic_slice_in_dim(sink_tensor, core * half + BLOCK * unit(w) + start, size, axis=1)

    outward = lambda v: lax.ppermute(v, "ev", [(1, 0), (2, 3)])
    inward = lambda v: lax.ppermute(v, "ev", [(0, 1), (3, 2)])
    middle = lambda v: lax.ppermute(v, "ev", [(1, 2), (2, 1)])
    swap_chips = lambda v: lax.ppermute(v, "src", [(0, 2), (2, 0), (1, 3), (3, 1)])
    swap_cores = lambda v: lax.ppermute(v, "src", [(0, 1), (1, 0), (2, 3), (3, 2)])
    swap_groups = lambda v: lax.ppermute(v, "grp", [(0, 1), (1, 0)])

    table = jnp.asarray(relay_table(evs, units))
    table = lax.dynamic_index_in_dim(table, (ev * 4 + position) * 2 + grp, 0, keepdims=False)
    base1, base2, base3, base4, base5, base6 = BASES

    choose = lambda a, b: jnp.where(is_end, a, b)

    sent = rows_to_send(perambulators, source_times)
    rows_here = own_rows(sent, perambulators.shape[0], source_times)
    spins = rows_here.shape[0]
    own0 = own(0)
    rows_here = after(rows_here, own0, table)
    some = lax.dynamic_slice_in_dim(rows_here, grp * (spins // 2), spins // 2, axis=0)
    mine = jnp.stack([lax.ppermute(some, "ev", [(j, (j + k) % evs) for j in range(evs)]) for k in range(1, evs)])
    own1, own2a, own2b = own(1), own(2, 0, BLOCK // 2), own(2, BLOCK // 2, BLOCK // 2)
    others = swap_groups(after(mine, own1, own2a, own2b))
    whole_rows = jnp.where(grp == 0, jnp.concatenate([mine, others], 1), jnp.concatenate([others, mine], 1))
    whole_rows = [rows_here if k == 0 else whole_rows[k - 1] for k in range(evs)]
    turned = jnp.stack([whole_rows[(evs - 1 - k) % evs] for k in range(2 * evs - 1)])
    turned = lax.dynamic_slice_in_dim(turned, evs - 1 - ev, evs, axis=0)
    per_time = turned.transpose(1, 2, 0, 3, 4).reshape(spins, 2, n, n)
    other_time = swap_cores(per_time)
    source = source_tensor[0]
    other_source = swap_cores(after(source, rows_here))
    *lefts, w, q, q_near = maps(
        [per_time, other_time], spin_index, core * half, evs, half, slice_a, e, [ev * e, near * e]
    )
    own0, own1 = after((own0, own1), mine)
    b1, q1, e2, b3 = middle(own0), outward(own0), inward(own0), middle(own1)
    acc = jnp.zeros((2 * structures, 2, n // LANES, 8, LANES), F32)

    block = near * units + 1 + grp
    t_own, to_near = project_source(lefts[0], source, structures, block, None, 0)
    b1, q1 = after((b1, q1), t_own)
    q2 = outward(b1)
    out1 = choose(q1, b1)
    x1 = swap_chips(out1)
    e3, e1a, e1b = inward(after(own1, out1)), inward(after(own2a, out1)), inward(after(own2b, out1))
    t_other, to_near = project_source(lefts[1], after(other_source, t_own, b1, q1, out1), structures, block, to_near, 1)
    ts = (t_own, t_other)
    b2 = middle(after(e2, t_other))
    near_t = inward(after(to_near, t_other))
    acc = contract(sink_tensor, ts, table, 0, q, w, after(acc, e2), 1)
    q3 = outward(after(b3, acc))
    out2 = choose(after(q2, acc), e2)
    x2 = swap_chips(out2)
    acc = contract(sink_tensor, ts, table, 6, q, w, after(acc, b3, out2, x1), units // 2)
    acc = contract_slots([[(q1,)], [(b1,)], [(x1,)]], ts, table, base1, q, w, acc)
    q4 = outward(after(b2, acc))
    b4 = middle(after(e3, acc))
    out3 = choose(after(q3, acc), b3)
    x3 = swap_chips(out3)
    far_t = swap_groups(after(near_t, acc))
    acc = contract_slots([[(q2,), (e2,)], [(b3,)]], ts, table, base2, q, w, after(acc, b2, e3, out3, near_t))
    b5 = middle(after(e1a, acc))
    acc = contract_slots([[(x2,)], [(q3,), (e3,)]], ts, table, base3, q, w, after(acc, e1a))
    q5 = outward(after(b4, acc))
    out4 = choose(after(q4, acc), b2)
    x4 = swap_chips(out4)
    acc = contract_slots([[(q4,), (b2,)], [(x3,)], [(e1a, e1b)]], ts, table, base4, q, w, after(acc, b4, out4))
    q6 = outward(after(b5, acc))
    acc = contract_near(sink_tensor, near_t, far_t, table, 9, q_near, w, after(acc, b5))
    out5 = choose(after(q5, acc), b4)[:, BLOCK // 2 :]
    x5 = swap_chips(out5)
    acc = contract_slots([[(x4,)], [(q5,), (b4,)]], ts, table, base5, q, w, after(acc, out5))
    acc = contract(sink_tensor, ts, table, 3, q, w, acc, 1)
    acc = contract_slots([[(q6, x5), (b5, x5)]], ts, table, base6, q, w, acc)

    part = acc.sum((2, 3, 4)).reshape(2, structures, 2)
    total = part[0] + swap_cores(part[1])
    return sum((lax.ppermute(total, "ev", [(j, (j + k) % evs) for j in range(evs)]) for k in range(1, evs)), total)


def body(relay, *args):
    totals = (body_relay if relay else body_any)(*args)
    return (totals * float(args[0].shape[3]) ** -1.5)[None]


def solution(mesh):
    relay = mesh.shape["ev"] == 4 and mesh.shape["src"] == 4 and mesh.shape["grp"] == 2
    in_specs = (
        P("grp", "ev", None, None),
        P("src", None, None, "ev", None),
        P("src", None, None, "ev", None),
        P(),
        P(),
    )
    out_specs = P("src", "grp", None)
    return jax.shard_map(functools.partial(body, relay), mesh=mesh, in_specs=in_specs, out_specs=out_specs, check_vma=False)
```
